128 devices in a mesh: region: 16 (over z_hi, y, core), member: 8 (over z_lo, x).
Axes of the slice: x: 4, y: 4, z: 4 (z_hi: 2, z_lo: 2; z = z_hi * 2 + z_lo), core: 2. Of those that a mesh axis runs over, the one named last changes fastest.
Arguments:
- controls: float32 [16, 8, 256, 512], P('member', None, 'region'), may hold values from -6 to 6
- perturbations: float32 [64, 8, 256, 512], P('member', None, 'region'), may hold values from -1.5 to 1.5
- assignment: int32 [64], replicated, may hold values from 0 to 15
- courant: float32 [4, 4, 8, 256, 512], P(None, None, 'member', 'region'), may hold values from 0.02 to 0.24
- innovation: float32 [8, 256, 512], P('member', 'region'), may hold values from -6 to 6
- obs_weight: float32 [8, 256, 512], P('member', 'region'), may hold values from 0.3 to 3
Outputs:
- gradient: float32 [16, 8, 256, 512], P('member', None, 'region')
- departure: float32 [8, 256, 512], P('member', 'region')
The draws below stay inside these ranges and needn't reach their ends.
All inputs are finite; a program needn't handle non-finite values.
Results may differ from the reference program's by a relative error of at most 0.0001.
Values sent between devices are 32-bit elements; how exact they have to be, the bound alone decides.
A program may use at most 64 MiB of HBM per device.

```python
import math
import jax
import jax.numpy as jnp
from jax import lax

NY = 512
NZ = 8
FIELDS = 16
MEMBERS = 64
PASSES = 16
STEPS = 4
NX = 256


def place_ends(result, stream_key, smallest, high):
    extent = result.shape
    index_at = [jax.random.randint(jax.random.fold_in(stream_key, axis), (), 0, extent[axis]) for axis in range(len(extent))]
    result = result.at[tuple(index_at)].set(smallest)
    longest = extent.index(max(extent))
    index_at[longest] = (index_at[longest] + 1) % extent[longest]
    return result.at[tuple(index_at)].set(high)


def block_scale(rng, extent, pieces, smallest, top_value):
    def one(dim, shards_of):
        draws = jax.random.uniform(jax.random.fold_in(jax.random.fold_in(rng, 6), dim), (shards_of,), jnp.float32, smallest / len(pieces), top_value / len(pieces))
        return jnp.repeat(jnp.exp(draws), extent[dim] // shards_of).reshape((-1,) + (1,) * (len(extent) - dim - 1))

    gain = one(*pieces[0])
    for cut in pieces[1:]:
        gain = gain * one(*cut)
    return gain


def centred(rng, extent, spread, bound, cuts=(), held_as=jnp.bfloat16):
    drawn = jax.random.normal(rng, extent, jnp.float32) * spread
    if len(cuts) > 0:
        drawn = block_scale(rng, extent, cuts, -0.22, 0.18) * drawn
    return jnp.clip(drawn, min=-bound, max=bound).astype(held_as)


def setup_inputs(seed: int = 0) -> dict:
    splits = jax.random.split(jax.random.key(seed), 7)
    controls = centred(splits[0], (FIELDS, NZ, NX, NY), 1.0, 6.0, ((0, 8), (2, 16)), jnp.float32)
    perturbations = centred(splits[1], (MEMBERS, NZ, NX, NY), 0.25, 1.5, ((0, 8), (2, 16)), jnp.float32)
    assignment = place_ends(jax.random.randint(splits[2], (MEMBERS,), 0, FIELDS), jax.random.fold_in(splits[2], 1), 0, FIELDS - 1).astype(jnp.int32)
    courant = jnp.clip(0.02 + 0.22 * jax.random.uniform(splits[3], (STEPS, 4, NZ, NX, NY), jnp.float32) ** block_scale(splits[3], (STEPS, 4, NZ, NX, NY), ((2, 8), (3, 16)), -0.2, 0.2), 0.02, 0.24)
    innovation = centred(splits[4], (NZ, NX, NY), 1.0, 6.0, ((0, 8), (1, 16)), jnp.float32)
    obs_weight = jnp.clip(jnp.exp(math.log(3.0) - 2.3025851 * jax.random.uniform(splits[5], (NZ, NX, NY), jnp.float32) ** block_scale(splits[5], (NZ, NX, NY), ((0, 8), (1, 16)), -0.2, 0.2)), 0.3, 3.0)
    return dict(controls=controls, perturbations=perturbations, assignment=assignment, courant=courant, innovation=innovation, obs_weight=obs_weight)


def smooth(fields):
    for repeat in range(PASSES):
        padded = jnp.pad(fields, ((0, 0), (0, 0), (1, 1), (1, 1)))
        beside_all = padded[:, :, 2:, 1:-1] + padded[:, :, :-2, 1:-1] + padded[:, :, 1:-1, 2:] + padded[:, :, 1:-1, :-2]
        fields = fields + 0.2 * (beside_all - 4.0 * fields)
    return fields

def transport(state, courant):
    for step in range(STEPS):
        coeffs = courant[step]
        padded = jnp.pad(state, ((0, 0), (1, 1), (1, 1)))
        center = 1.0 - lax.optimization_barrier(jnp.sum(coeffs, 0))
        state = center * state + coeffs[0] * padded[:, :-2, 1:-1] + coeffs[1] * padded[:, 2:, 1:-1] + coeffs[2] * padded[:, 1:-1, :-2] + coeffs[3] * padded[:, 1:-1, 2:]
    return state

def reference(controls, perturbations, assignment, courant, innovation, obs_weight):
    one_hot = (assignment[:, None] == jnp.arange(FIELDS, dtype=jnp.int32)[None, :]).astype(jnp.float32)
    smoothed = smooth(controls)
    member_sums = jnp.einsum('kl,kzxy->lzxy', one_hot, perturbations, precision=lax.Precision.HIGHEST)
    increment = lax.optimization_barrier(jnp.sum(smoothed * member_sums, 0))
    moved, pull_back = jax.vjp(lambda value: transport(value, courant), increment)
    departure = obs_weight * (moved - innovation)
    adjoint = pull_back(departure)[0]
    field_terms = jnp.einsum('kl,kzxy->lzxy', one_hot, perturbations * adjoint[None], precision=lax.Precision.HIGHEST)
    gradient = controls + smooth(field_terms)
    return (gradient, departure)
```

```python
import functools

import jax
import jax.numpy as jnp
import numpy as np
from jax import lax
from jax.experimental import pallas as pl
from jax.experimental.pallas import tpu as pltpu
from jax.sharding import PartitionSpec as P

PASSES = 16
STEPS = 4
GROUP = 8
HALO = 8
MESH = pl.DeviceIdType.MESH
F32 = jnp.float32
BF16 = jnp.bfloat16


def tables(columns):
    index = np.arange(1, columns + 1, dtype=np.float64)
    sine = np.sqrt(2.0 / (columns + 1)) * np.sin(np.pi * np.outer(index, index) / (columns + 1))
    high = sine.astype(BF16)
    low = (sine - high.astype(np.float64)).astype(BF16)
    center = (1.0 + 2.0 * np.cos(np.pi * index / (columns + 1))) / 5.0
    power = np.ones((1, columns))
    for _ in range(PASSES):
        wider = np.zeros((power.shape[0] + 2, columns))
        wider[1:-1] += center * power
        wider[2:] += power / 5.0
        wider[:-2] += power / 5.0
        power = wider
    coef = np.broadcast_to(power[PASSES:, None, :], (PASSES + 1, GROUP, columns))
    return high, low, np.ascontiguousarray(coef).astype(np.float32)


def split(x):
    high = x.astype(BF16)
    return high, (x - high.astype(F32)).astype(BF16)


def times_sine(x, vhi, vlo):
    high, low = split(x)
    out = jnp.dot(high, vhi[...], preferred_element_type=F32)
    out += jnp.dot(low, vhi[...], preferred_element_type=F32)
    out += jnp.dot(high, vlo[...], preferred_element_type=F32)
    return out


def kernel(
    regions, ctl, pert, assign, cour, innov, weight, vhi_in, vlo_in, coef_in,
    lft, dep_out,
    vhi, vlo, coef, ctl3, pbuf, smo_out, smo, ms, inc, cour_x, inn_x, wgt_x, adj, dep, modes, rows, mid, fin,
    load_sem, pert_send, pert_recv, nb_send, nb_recv, smo_send, smo_recv, fin_send, fin_recv, out_sem,
):
    r, me = lax.axis_index("region"), lax.axis_index("member")
    fl, levels, height, columns = ctl.shape
    kl = pert.shape[0]
    fields = fl * levels
    groups = fields // GROUP
    last = regions - 1

    barrier = pltpu.get_barrier_semaphore()

    def peer(d):
        return lax.rem(me + d, levels)

    for d in range(1, levels):
        pl.semaphore_signal(barrier, inc=1, device_id=(r, peer(d)), device_id_type=MESH)

    @pl.when(r > 0)
    def _():
        pl.semaphore_signal(barrier, inc=1, device_id=(r - 1, me), device_id_type=MESH)

    @pl.when(r < last)
    def _():
        pl.semaphore_signal(barrier, inc=1, device_id=(r + 1, me), device_id_type=MESH)

    loads = [
        pltpu.make_async_copy(vhi_in, vhi, load_sem.at[0]),
        pltpu.make_async_copy(vlo_in, vlo, load_sem.at[1]),
        pltpu.make_async_copy(coef_in, coef, load_sem.at[2]),
        pltpu.make_async_copy(ctl, ctl3.at[1], load_sem.at[3]),
        pltpu.make_async_copy(pert.at[:, me], pbuf.at[pl.ds(me * kl, kl)], load_sem.at[4]),
        pltpu.make_async_copy(cour.at[:, :, 0], cour_x.at[:, :, pl.ds(HALO, height)], load_sem.at[5]),
        pltpu.make_async_copy(innov.at[0], inn_x.at[pl.ds(HALO, height)], load_sem.at[6]),
        pltpu.make_async_copy(weight.at[0], wgt_x.at[pl.ds(HALO, height)], load_sem.at[7]),
    ]
    for copy in loads:
        copy.start()

    top, bottom = pl.ds(0, HALO), pl.ds(height - HALO, HALO)
    above, below = pl.ds(0, HALO), pl.ds(HALO + height, HALO)
    nb = [
        ((ctl, ctl3.at[0]), (ctl, ctl3.at[2])),
        ((cour.at[:, :, 0, bottom], cour_x.at[:, :, above]), (cour.at[:, :, 0, top], cour_x.at[:, :, below])),
        ((innov.at[0, bottom], inn_x.at[above]), (innov.at[0, top], inn_x.at[below])),
        ((weight.at[0, bottom], wgt_x.at[above]), (weight.at[0, top], wgt_x.at[below])),
        ((ms.at[1], ms.at[0]), (ms.at[1], ms.at[2])),
        ((inc.at[pl.ds(height, HALO)], inc.at[above]), (inc.at[pl.ds(HALO, HALO)], inc.at[below])),
        ((adj.at[1], adj.at[0]), (adj.at[1], adj.at[2])),
    ]

    def to_neighbour(number, up):
        src, dst = nb[number][up]
        return pltpu.make_async_remote_copy(
            src_ref=src, dst_ref=dst, send_sem=nb_send.at[number, up], recv_sem=nb_recv.at[number, up],
            device_id=(r - 1 if up else r + 1, me), device_id_type=MESH,
        )

    def exchange(number):
        @pl.when(r < last)
        def _():
            to_neighbour(number, 0).start()

        @pl.when(r > 0)
        def _():
            to_neighbour(number, 1).start()

    def arrived(number):
        @pl.when(r > 0)
        def _():
            to_neighbour(number, 0).wait_recv()

        @pl.when(r < last)
        def _():
            to_neighbour(number, 1).wait_recv()

    def sent(number):
        @pl.when(r < last)
        def _():
            to_neighbour(number, 0).wait_send()

        @pl.when(r > 0)
        def _():
            to_neighbour(number, 1).wait_send()

    def pert_copy(to, source):
        return pltpu.make_async_remote_copy(
            src_ref=pert.at[:, to], dst_ref=pbuf.at[pl.ds(source * kl, kl)],
            send_sem=pert_send.at[to], recv_sem=pert_recv.at[source],
            device_id=(r, to), device_id_type=MESH,
        )

    neighbours = (r > 0).astype(jnp.int32) + (r < last).astype(jnp.int32)
    pl.semaphore_wait(barrier, levels - 1 + neighbours)

    exchange(0)
    for d in range(1, levels):
        pert_copy(peer(d), me).start()
    for number in (1, 2, 3):
        exchange(number)

    @pl.when(r == 0)
    def _():
        for ref in (inn_x, wgt_x, inc):
            ref[0:HALO] = jnp.zeros((HALO, columns), F32)
        cour_x[:, :, 0:HALO] = jnp.zeros((STEPS, 4, HALO, columns), F32)

    @pl.when(r == last)
    def _():
        for ref in (inn_x, wgt_x, inc):
            ref[HALO + height :] = jnp.zeros((HALO, columns), F32)
        cour_x[:, :, HALO + height :] = jnp.zeros((STEPS, 4, HALO, columns), F32)

    def smooth(x, keep):
        flat = jnp.concatenate([part.reshape(GROUP * height, columns) for part in x], axis=0)
        spectrum = times_sine(flat, vhi, vlo)
        for t in range(columns // 128):
            lane = slice(t * 128, (t + 1) * 128)
            modes[t] = spectrum[:, lane]
            for part in range(3):
                for i in range(height):
                    rows[part * height + i, :, lane] = modes[t, pl.ds(part * GROUP * height + i, GROUP, stride=height), :]

        @pl.when(r == 0)
        def _():
            rows[height - 1] = jnp.zeros((GROUP, columns), F32)
            for k in range(1, height):
                rows[height - 1 - k] = -rows[height - 1 + k]

        @pl.when(r == last)
        def _():
            rows[2 * height] = jnp.zeros((GROUP, columns), F32)
            for k in range(1, height):
                rows[2 * height + k] = -rows[2 * height - k]

        step = 4
        tiles = columns // 128

        @pl.loop(0, tiles * (height // step))
        def _(it):
            t = lax.rem(it, tiles)
            lane = pl.ds(pl.multiple_of(t * 128, 128), 128)
            i = (it // tiles) * step
            g = [rows[i + j, :, lane] for j in range(2 * PASSES + step)]
            total = [None] * step
            for d in range(PASSES + 1):
                c = coef[d, :, lane]
                for j in range(step):
                    at = PASSES + j
                    term = c * g[at] if d == 0 else c * (g[at - d] + g[at + d])
                    total[j] = term if d == 0 else total[j] + term
            for j in range(step):
                mid[t, pl.ds(i + j, GROUP, stride=height), :] = total[j]

        keep(times_sine(jnp.concatenate([mid[t] for t in range(tiles)], axis=1), vhi, vlo))

    for number in (0, 1, 2, 3):
        loads[number].wait()
    arrived(0)

    def smo_copy(plane, field, level, source):
        return pltpu.make_async_remote_copy(
            src_ref=smo_out.at[plane], dst_ref=smo.at[source * fl + field],
            send_sem=smo_send.at[plane], recv_sem=smo_recv.at[source, field],
            device_id=(r, level), device_id_type=MESH,
        )

    def smo_own(plane, field):
        return pltpu.make_async_copy(smo_out.at[plane], smo.at[me * fl + field], smo_send.at[plane])

    for q in range(groups):
        parts = [
            jnp.concatenate([ctl3[part, (q * GROUP + j) // levels, (q * GROUP + j) % levels][None] for j in range(GROUP)])
            for part in range(3)
        ]

        def keep(result, q=q):
            smo_out[q * GROUP : (q + 1) * GROUP] = result.reshape(GROUP, height, columns)

        smooth(parts, keep)
        for j in range(GROUP):
            plane = q * GROUP + j
            field, level = plane // levels, plane % levels

            @pl.when(me != level)
            def _():
                smo_copy(plane, field, level, me).start()

            @pl.when(me == level)
            def _():
                smo_own(plane, field).start()

    loads[4].wait()
    tiles = columns // 128

    def add_source(source, first):
        which = [assign[source * kl + k] for k in range(kl)]

        @pl.loop(0, (height // 8) * tiles)
        def _(it):
            lane = pl.ds(pl.multiple_of(lax.rem(it, tiles) * 128, 128), 128)
            row = pl.ds(pl.multiple_of((it // tiles) * 8, 8), 8)
            p = [pbuf[source * kl + k, row, lane] for k in range(kl)]
            for l in range(fields):
                terms = [jnp.where(which[k] == l, 1.0, 0.0) * p[k] for k in range(kl)]
                while len(terms) > 1:
                    terms = [a + b for a, b in zip(terms[::2], terms[1::2])]
                ms[1, l, row, lane] = terms[0] if first else ms[1, l, row, lane] + terms[0]

    add_source(me, True)
    for d in range(1, levels):
        source = peer(levels - d)
        pert_copy(source, source).wait_recv()
        add_source(source, False)
    exchange(4)

    for d in range(levels):
        source = peer(d)
        for field in range(fl):
            if d == 0:
                smo_own(field * levels + me, field).wait()
            else:
                smo_copy(field * levels + me, field, me, source).wait_recv()

    total = smo[0] * ms[1, 0]
    for l in range(1, fields):
        total += smo[l] * ms[1, l]
    inc[HALO : HALO + height] = total
    exchange(5)
    for number in (5, 6, 7):
        loads[number].wait()
    for number in (1, 2, 3, 5):
        arrived(number)

    extent = height + 2 * HALO
    column = lax.broadcasted_iota(jnp.int32, (extent, columns), 1)

    def from_west(y):
        return jnp.where(column == 0, 0.0, pltpu.roll(y, 1, 1))

    def from_east(y):
        return jnp.where(column == columns - 1, 0.0, pltpu.roll(y, columns - 1, 1))

    def from_north(y):
        return pltpu.roll(y, 1, 0)

    def from_south(y):
        return pltpu.roll(y, extent - 1, 0)

    state = inc[...]
    for s in range(STEPS):
        n, so, w, e = (cour_x[s, k] for k in range(4))
        state = (
            (1.0 - (n + so + w + e)) * state
            + n * from_north(state) + so * from_south(state) + w * from_west(state) + e * from_east(state)
        )
    state = wgt_x[...] * (state - inn_x[...])
    dep[...] = state[HALO : HALO + height]
    dep_copy = pltpu.make_async_copy(dep, dep_out.at[0], out_sem)
    dep_copy.start()
    for s in range(STEPS - 1, -1, -1):
        n, so, w, e = (cour_x[s, k] for k in range(4))
        state = (
            (1.0 - (n + so + w + e)) * state
            + from_south(n * state) + from_north(so * state) + from_east(w * state) + from_west(e * state)
        )
    adj[1] = state[HALO : HALO + height]
    exchange(6)
    arrived(4)
    arrived(6)

    def fin_copy(owner, level):
        return pltpu.make_async_remote_copy(
            src_ref=fin.at[pl.ds(owner * fl, fl)], dst_ref=lft.at[:, level],
            send_sem=fin_send.at[owner], recv_sem=fin_recv.at[level],
            device_id=(r, owner), device_id_type=MESH,
        )

    def fin_own():
        return pltpu.make_async_copy(fin.at[pl.ds(me * fl, fl)], lft.at[:, me], fin_send.at[me])

    for q in range(groups):
        parts = [ms[part, q * GROUP : (q + 1) * GROUP] * adj[part][None] for part in range(3)]

        def keep(result, q=q):
            fin[q * GROUP : (q + 1) * GROUP] = result.reshape(GROUP, height, columns)

        smooth(parts, keep)
        for owner in range(q * GROUP // fl, (q + 1) * GROUP // fl):
            @pl.when(me != owner)
            def _():
                fin_copy(owner, me).start()

            @pl.when(me == owner)
            def _():
                fin_own().start()

    for d in range(1, levels):
        pert_copy(peer(d), me).wait_send()
    for plane in range(fl * levels):
        @pl.when(me != plane % levels)
        def _():
            smo_copy(plane, plane // levels, plane % levels, me).wait_send()
    for number in range(len(nb)):
        sent(number)
    dep_copy.wait()
    fin_own().wait()
    for d in range(1, levels):
        fin_copy(peer(d), me).wait_send()
    for d in range(1, levels):
        fin_copy(me, peer(d)).wait_recv()


def solution(mesh):
    regions = mesh.shape["region"]

    def shards(controls, perturbations, assignment, courant, innovation, obs_weight):
        fl, levels, height, columns = controls.shape
        kl = perturbations.shape[0]
        fields = fl * levels
        vhi, vlo, coef = tables(columns)
        extent = height + 2 * HALO
        any_space = pl.BlockSpec(memory_space=pl.ANY)
        smem = pl.BlockSpec(memory_space=pltpu.SMEM)
        dma = pltpu.SemaphoreType.DMA
        lft, departure = pl.pallas_call(
            functools.partial(kernel, regions),
            out_shape=(
                jax.ShapeDtypeStruct(controls.shape, F32),
                jax.ShapeDtypeStruct(innovation.shape, F32),
            ),
            in_specs=[any_space, any_space, smem] + [any_space] * 6,
            out_specs=(any_space, any_space),
            scratch_shapes=[
                pltpu.VMEM((columns, columns), BF16),
                pltpu.VMEM((columns, columns), BF16),
                pltpu.VMEM((PASSES + 1, GROUP, columns), F32),
                pltpu.VMEM((3, fl, levels, height, columns), F32),
                pltpu.VMEM((kl * levels, height, columns), F32),
                pltpu.VMEM((fields, height, columns), F32),
                pltpu.VMEM((fields, height, columns), F32),
                pltpu.VMEM((3, fields, height, columns), F32),
                pltpu.VMEM((extent, columns), F32),
                pltpu.VMEM((STEPS, 4, extent, columns), F32),
                pltpu.VMEM((extent, columns), F32),
                pltpu.VMEM((extent, columns), F32),
                pltpu.VMEM((3, height, columns), F32),
                pltpu.VMEM((height, columns), F32),
                pltpu.VMEM((columns // 128, 3 * GROUP * height, 128), F32),
                pltpu.VMEM((3 * height, GROUP, columns), F32),
                pltpu.VMEM((columns // 128, GROUP * height, 128), F32),
                pltpu.VMEM((fields, height, columns), F32),
                dma((8,)),
                dma((levels,)),
                dma((levels,)),
                dma((7, 2)),
                dma((7, 2)),
                dma((fields,)),
                dma((levels, fl)),
                dma((levels,)),
                dma((levels,)),
                dma,
            ],
            compiler_params=pltpu.CompilerParams(
                collective_id=0, has_side_effects=True, vmem_limit_bytes=40 * 2**20
            ),
            cost_estimate=pl.CostEstimate(flops=2 * 10**9, bytes_accessed=8 * 2**20, transcendentals=0),
        )(controls, perturbations, assignment, courant, innovation, obs_weight, vhi, vlo, coef)
        return controls + lft, departure

    return jax.shard_map(
        shards,
        mesh=mesh,
        in_specs=(
            P("member", None, "region", None),
            P("member", None, "region", None),
            P(),
            P(None, None, "member", "region", None),
            P("member", "region", None),
            P("member", "region", None),
        ),
        out_specs=(P("member", None, "region", None), P("member", "region", None)),
        check_vma=False,
    )
```

```python
import functools

import jax
import jax.numpy as jnp
import numpy as np
from jax import lax
from jax.experimental import pallas as pl
from jax.experimental.pallas import tpu as pltpu
from jax.sharding import PartitionSpec as P

PASSES = 16
STEPS = 4
GROUP = 8
HALO = 8
MESH = pl.DeviceIdType.MESH
ORDER = ((1, 1), (3, 0), (2, 1), (0, 1), (2, 0), (3, 1), (1, 0))
F32 = jnp.float32
BF16 = jnp.bfloat16


def tables(columns):
    index = np.arange(1, columns + 1, dtype=np.float64)
    sine = np.sqrt(2.0 / (columns + 1)) * np.sin(np.pi * np.outer(index, index) / (columns + 1))
    high = sine.astype(BF16)
    low = (sine - high.astype(np.float64)).astype(BF16)
    center = (1.0 + 2.0 * np.cos(np.pi * index / (columns + 1))) / 5.0
    power = np.ones((1, columns))
    for _ in range(PASSES):
        wider = np.zeros((power.shape[0] + 2, columns))
        wider[1:-1] += center * power
        wider[2:] += power / 5.0
        wider[:-2] += power / 5.0
        power = wider
    coef = np.broadcast_to(power[PASSES:, None, :], (PASSES + 1, GROUP, columns))
    return high, low, np.ascontiguousarray(coef).astype(np.float32)


def split(x):
    high = x.astype(BF16)
    return high, (x - high.astype(F32)).astype(BF16)


def times_sine(x, vhi, vlo):
    high, low = split(x)
    out = jnp.dot(high, vhi[...], preferred_element_type=F32)
    out += jnp.dot(low, vhi[...], preferred_element_type=F32)
    out += jnp.dot(high, vlo[...], preferred_element_type=F32)
    return out


def kernel(
    regions, ctl, pert, assign, cour, innov, weight, vhi_in, vlo_in, coef_in,
    lft, dep_out,
    vhi, vlo, coef, ctl3, pbuf, smo_out, smo, ms, inc, cour_x, inn_x, wgt_x, adj, dep, modes, rows, mid, fin,
    load_sem, pert_send, pert_recv, nb_send, nb_recv, smo_send, smo_recv, fin_send, fin_recv, out_sem,
):
    r, me = lax.axis_index("region"), lax.axis_index("member")
    fl, levels, height, columns = ctl.shape
    kl = pert.shape[0]
    fields = fl * levels
    groups = fields // GROUP
    last = regions - 1

    barrier = pltpu.get_barrier_semaphore()

    xs = levels // 2
    order = [offset for offset in ORDER if offset[0] < xs]
    mx, mz = lax.rem(me, xs), me // xs

    def member(x, z):
        return lax.rem(mz + z, 2) * xs + lax.rem(mx + x, xs)

    targets = [member(x, z) for x, z in order]
    sources = [member(xs - x, z) for x, z in order]
    for to in targets:
        pl.semaphore_signal(barrier, inc=1, device_id=(r, to), device_id_type=MESH)

    @pl.when(r > 0)
    def _():
        pl.semaphore_signal(barrier, inc=1, device_id=(r - 1, me), device_id_type=MESH)

    @pl.when(r < last)
    def _():
        pl.semaphore_signal(barrier, inc=1, device_id=(r + 1, me), device_id_type=MESH)

    loads = [
        pltpu.make_async_copy(vhi_in, vhi, load_sem.at[0]),
        pltpu.make_async_copy(vlo_in, vlo, load_sem.at[1]),
        pltpu.make_async_copy(coef_in, coef, load_sem.at[2]),
        pltpu.make_async_copy(ctl, ctl3.at[1], load_sem.at[3]),
        pltpu.make_async_copy(pert.at[:, me], pbuf.at[pl.ds(me * kl, kl)], load_sem.at[4]),
        pltpu.make_async_copy(cour.at[:, :, 0], cour_x.at[:, :, pl.ds(HALO, height)], load_sem.at[5]),
        pltpu.make_async_copy(innov.at[0], inn_x.at[pl.ds(HALO, height)], load_sem.at[6]),
        pltpu.make_async_copy(weight.at[0], wgt_x.at[pl.ds(HALO, height)], load_sem.at[7]),
    ]
    for copy in loads:
        copy.start()

    top, bottom = pl.ds(0, HALO), pl.ds(height - HALO, HALO)
    above, below = pl.ds(0, HALO), pl.ds(HALO + height, HALO)
    nb = [
        ((ctl, ctl3.at[0]), (ctl, ctl3.at[2])),
        ((cour.at[:, :, 0, bottom], cour_x.at[:, :, above]), (cour.at[:, :, 0, top], cour_x.at[:, :, below])),
        ((innov.at[0, bottom], inn_x.at[above]), (innov.at[0, top], inn_x.at[below])),
        ((weight.at[0, bottom], wgt_x.at[above]), (weight.at[0, top], wgt_x.at[below])),
        ((ms.at[1, :, top], ms.at[0, :, top]), (ms.at[1, :, top], ms.at[2, :, top])),
        ((inc.at[pl.ds(height, HALO)], inc.at[above]), (inc.at[pl.ds(HALO, HALO)], inc.at[below])),
        ((adj.at[1], adj.at[0]), (adj.at[1], adj.at[2])),
        ((ms.at[1, :, bottom], ms.at[0, :, bottom]), (ms.at[1, :, bottom], ms.at[2, :, bottom])),
    ]

    def to_neighbour(number, up):
        src, dst = nb[number][up]
        return pltpu.make_async_remote_copy(
            src_ref=src, dst_ref=dst, send_sem=nb_send.at[number, up], recv_sem=nb_recv.at[number, up],
            device_id=(r - 1 if up else r + 1, me), device_id_type=MESH,
        )

    def exchange(number):
        @pl.when(r < last)
        def _():
            to_neighbour(number, 0).start()

        @pl.when(r > 0)
        def _():
            to_neighbour(number, 1).start()

    def arrived(number):
        @pl.when(r > 0)
        def _():
            to_neighbour(number, 0).wait_recv()

        @pl.when(r < last)
        def _():
            to_neighbour(number, 1).wait_recv()

    def sent(number):
        @pl.when(r < last)
        def _():
            to_neighbour(number, 0).wait_send()

        @pl.when(r > 0)
        def _():
            to_neighbour(number, 1).wait_send()

    halves = (top, bottom)

    def pert_copy(to, source, half):
        return pltpu.make_async_remote_copy(
            src_ref=pert.at[:, to, halves[half]], dst_ref=pbuf.at[pl.ds(source * kl, kl), halves[half]],
            send_sem=pert_send.at[to, half], recv_sem=pert_recv.at[source, half],
            device_id=(r, to), device_id_type=MESH,
        )

    neighbours = (r > 0).astype(jnp.int32) + (r < last).astype(jnp.int32)
    pl.semaphore_wait(barrier, levels - 1 + neighbours)

    exchange(0)
    for half in range(2):
        for to in targets:
            pert_copy(to, me, half).start()
    for number in (1, 2, 3):
        exchange(number)

    @pl.when(r == 0)
    def _():
        for ref in (inn_x, wgt_x, inc):
            ref[0:HALO] = jnp.zeros((HALO, columns), F32)
        cour_x[:, :, 0:HALO] = jnp.zeros((STEPS, 4, HALO, columns), F32)

    @pl.when(r == last)
    def _():
        for ref in (inn_x, wgt_x, inc):
            ref[HALO + height :] = jnp.zeros((HALO, columns), F32)
        cour_x[:, :, HALO + height :] = jnp.zeros((STEPS, 4, HALO, columns), F32)

    def smooth(x, keep):
        flat = jnp.concatenate([part.reshape(GROUP * height, columns) for part in x], axis=0)
        spectrum = times_sine(flat, vhi, vlo)
        for t in range(columns // 128):
            lane = slice(t * 128, (t + 1) * 128)
            modes[t] = spectrum[:, lane]
            for part in range(3):
                for i in range(height):
                    rows[part * height + i, :, lane] = modes[t, pl.ds(part * GROUP * height + i, GROUP, stride=height), :]

        @pl.when(r == 0)
        def _():
            rows[height - 1] = jnp.zeros((GROUP, columns), F32)
            for k in range(1, height):
                rows[height - 1 - k] = -rows[height - 1 + k]

        @pl.when(r == last)
        def _():
            rows[2 * height] = jnp.zeros((GROUP, columns), F32)
            for k in range(1, height):
                rows[2 * height + k] = -rows[2 * height - k]

        step = 4
        tiles = columns // 128

        @pl.loop(0, tiles * (height // step))
        def _(it):
            t = lax.rem(it, tiles)
            lane = pl.ds(pl.multiple_of(t * 128, 128), 128)
            i = (it // tiles) * step
            g = [rows[i + j, :, lane] for j in range(2 * PASSES + step)]
            total = [None] * step
            for d in range(PASSES + 1):
                c = coef[d, :, lane]
                for j in range(step):
                    at = PASSES + j
                    term = c * g[at] if d == 0 else c * (g[at - d] + g[at + d])
                    total[j] = term if d == 0 else total[j] + term
            for j in range(step):
                mid[t, pl.ds(i + j, GROUP, stride=height), :] = total[j]

        keep(times_sine(jnp.concatenate([mid[t] for t in range(tiles)], axis=1), vhi, vlo))

    def add_source(source, half, first):
        which = [assign[source * kl + k] for k in range(kl)]
        p = [pbuf[source * kl + k, halves[half]] for k in range(kl)]
        for l in range(fields):
            terms = [jnp.where(which[k] == l, 1.0, 0.0) * p[k] for k in range(kl)]
            while len(terms) > 1:
                terms = [a + b for a, b in zip(terms[::2], terms[1::2])]
            ms[1, l, halves[half]] = terms[0] if first else ms[1, l, halves[half]] + terms[0]

    loads[4].wait()
    for half in range(2):
        add_source(me, half, True)

    for number in (0, 1, 2, 3):
        loads[number].wait()
    arrived(0)

    def smo_copy(plane, field, level, source):
        return pltpu.make_async_remote_copy(
            src_ref=smo_out.at[plane], dst_ref=smo.at[source * fl + field],
            send_sem=smo_send.at[plane], recv_sem=smo_recv.at[source, field],
            device_id=(r, level), device_id_type=MESH,
        )

    def smo_own(plane, field):
        return pltpu.make_async_copy(smo_out.at[plane], smo.at[me * fl + field], smo_send.at[plane])

    for q in range(groups):
        parts = [
            jnp.concatenate([ctl3[part, (q * GROUP + j) // levels, (q * GROUP + j) % levels][None] for j in range(GROUP)])
            for part in range(3)
        ]

        def keep(result, q=q):
            smo_out[q * GROUP : (q + 1) * GROUP] = result.reshape(GROUP, height, columns)

        smooth(parts, keep)
        for field in range(q * GROUP // levels, (q + 1) * GROUP // levels):
            for to in targets:
                smo_copy(field * levels + to, field, to, me).start()
            smo_own(field * levels + me, field).start()

    for half in range(2):
        for source in sources:
            pert_copy(source, source, half).wait_recv()
            add_source(source, half, False)
        exchange((4, 7)[half])

    for field in range(fl):
        smo_own(field * levels + me, field).wait()
        for source in sources:
            smo_copy(field * levels + me, field, me, source).wait_recv()

    total = smo[0] * ms[1, 0]
    for l in range(1, fields):
        total += smo[l] * ms[1, l]
    inc[HALO : HALO + height] = total
    exchange(5)
    for number in (5, 6, 7):
        loads[number].wait()
    for number in (1, 2, 3, 5):
        arrived(number)

    extent = height + 2 * HALO
    column = lax.broadcasted_iota(jnp.int32, (extent, columns), 1)

    def from_west(y):
        return jnp.where(column == 0, 0.0, pltpu.roll(y, 1, 1))

    def from_east(y):
        return jnp.where(column == columns - 1, 0.0, pltpu.roll(y, columns - 1, 1))

    def from_north(y):
        return pltpu.roll(y, 1, 0)

    def from_south(y):
        return pltpu.roll(y, extent - 1, 0)

    state = inc[...]
    for s in range(STEPS):
        n, so, w, e = (cour_x[s, k] for k in range(4))
        state = (
            (1.0 - (n + so + w + e)) * state
            + n * from_north(state) + so * from_south(state) + w * from_west(state) + e * from_east(state)
        )
    state = wgt_x[...] * (state - inn_x[...])
    dep[...] = state[HALO : HALO + height]
    dep_copy = pltpu.make_async_copy(dep, dep_out.at[0], out_sem)
    dep_copy.start()
    for s in range(STEPS - 1, -1, -1):
        n, so, w, e = (cour_x[s, k] for k in range(4))
        state = (
            (1.0 - (n + so + w + e)) * state
            + from_south(n * state) + from_north(so * state) + from_east(w * state) + from_west(e * state)
        )
    adj[1] = state[HALO : HALO + height]
    exchange(6)
    for number in (4, 7, 6):
        arrived(number)

    def fin_copy(owner, level):
        return pltpu.make_async_remote_copy(
            src_ref=fin.at[pl.ds(owner * fl, fl)], dst_ref=lft.at[:, level],
            send_sem=fin_send.at[owner], recv_sem=fin_recv.at[level],
            device_id=(r, owner), device_id_type=MESH,
        )

    def fin_own():
        return pltpu.make_async_copy(fin.at[pl.ds(me * fl, fl)], lft.at[:, me], fin_send.at[me])

    for q in range(groups):
        begin = lax.rem(mz + 1 + q, 2) * GROUP if groups == 2 else q * GROUP
        parts = [ms[part, pl.ds(begin, GROUP)] * adj[part][None] for part in range(3)]

        def keep(result, begin=begin):
            fin[pl.ds(begin, GROUP)] = result.reshape(GROUP, height, columns)

        smooth(parts, keep)
        for (x, z), to in zip(order, targets):
            if groups == 1 or z == 1 - q:
                fin_copy(to, me).start()
        if q == groups - 1:
            fin_own().start()

    for to in targets:
        for half in range(2):
            pert_copy(to, me, half).wait_send()
        for field in range(fl):
            smo_copy(field * levels + to, field, to, me).wait_send()
    for number in range(len(nb)):
        sent(number)
    dep_copy.wait()
    fin_own().wait()
    for to in targets:
        fin_copy(to, me).wait_send()
    for source in sources:
        fin_copy(me, source).wait_recv()


def solution(mesh):
    regions = mesh.shape["region"]

    def shards(controls, perturbations, assignment, courant, innovation, obs_weight):
        fl, levels, height, columns = controls.shape
        kl = perturbations.shape[0]
        fields = fl * levels
        vhi, vlo, coef = tables(columns)
        extent = height + 2 * HALO
        any_space = pl.BlockSpec(memory_space=pltpu.HBM)
        smem = pl.BlockSpec(memory_space=pltpu.SMEM)
        dma = pltpu.SemaphoreType.DMA
        lft, departure = pl.pallas_call(
            functools.partial(kernel, regions),
            out_shape=(
                jax.ShapeDtypeStruct(controls.shape, F32),
                jax.ShapeDtypeStruct(innovation.shape, F32),
            ),
            in_specs=[any_space, any_space, smem] + [any_space] * 6,
            out_specs=(any_space, any_space),
            scratch_shapes=[
                pltpu.VMEM((columns, columns), BF16),
                pltpu.VMEM((columns, columns), BF16),
                pltpu.VMEM((PASSES + 1, GROUP, columns), F32),
                pltpu.VMEM((3, fl, levels, height, columns), F32),
                pltpu.VMEM((kl * levels, height, columns), F32),
                pltpu.VMEM((fields, height, columns), F32),
                pltpu.VMEM((fields, height, columns), F32),
                pltpu.VMEM((3, fields, height, columns), F32),
                pltpu.VMEM((extent, columns), F32),
                pltpu.VMEM((STEPS, 4, extent, columns), F32),
                pltpu.VMEM((extent, columns), F32),
                pltpu.VMEM((extent, columns), F32),
                pltpu.VMEM((3, height, columns), F32),
                pltpu.VMEM((height, columns), F32),
                pltpu.VMEM((columns // 128, 3 * GROUP * height, 128), F32),
                pltpu.VMEM((3 * height, GROUP, columns), F32),
                pltpu.VMEM((columns // 128, GROUP * height, 128), F32),
                pltpu.VMEM((fields, height, columns), F32),
                dma((8,)),
                dma((levels, 2)),
                dma((levels, 2)),
                dma((8, 2)),
                dma((8, 2)),
                dma((fields,)),
                dma((levels, fl)),
                dma((levels,)),
                dma((levels,)),
                dma,
            ],
            compiler_params=pltpu.CompilerParams(
                collective_id=0, has_side_effects=True, vmem_limit_bytes=56 * 2**20
            ),
            cost_estimate=pl.CostEstimate(flops=2 * 10**9, bytes_accessed=8 * 2**20, transcendentals=0),
        )(controls, perturbations, assignment, courant, innovation, obs_weight, vhi, vlo, coef)
        return controls + lft, departure

    return jax.shard_map(
        shards,
        mesh=mesh,
        in_specs=(
            P("member", None, "region", None),
            P("member", None, "region", None),
            P(),
            P(None, None, "member", "region", None),
            P("member", "region", None),
            P("member", "region", None),
        ),
        out_specs=(P("member", None, "region", None), P("member", "region", None)),
        check_vma=False,
    )
```

```python
import functools

import jax
import jax.numpy as jnp
import numpy as np
from jax import lax
from jax.experimental import pallas as pl
from jax.experimental.pallas import tpu as pltpu
from jax.sharding import PartitionSpec as P

PASSES = 16
STEPS = 4
GROUP = 8
HALO = 8
MESH = pl.DeviceIdType.MESH
BESIDE = (1, 3, 2)
F32 = jnp.float32
BF16 = jnp.bfloat16


def tables(columns):
    index = np.arange(1, columns + 1, dtype=np.float64)
    sine = np.sqrt(2.0 / (columns + 1)) * np.sin(np.pi * np.outer(index, index) / (columns + 1))
    high = sine.astype(BF16)
    low = (sine - high.astype(np.float64)).astype(BF16)
    center = (1.0 + 2.0 * np.cos(np.pi * index / (columns + 1))) / 5.0
    power = np.ones((1, columns))
    for _ in range(PASSES):
        wider = np.zeros((power.shape[0] + 2, columns))
        wider[1:-1] += center * power
        wider[2:] += power / 5.0
        wider[:-2] += power / 5.0
        power = wider
    coef = np.broadcast_to(power[PASSES:, None, :], (PASSES + 1, GROUP, columns))
    return high, low, np.ascontiguousarray(coef).astype(np.float32)


def split(x):
    high = x.astype(BF16)
    return high, (x - high.astype(F32)).astype(BF16)


def times_sine(x, vhi, vlo):
    high, low = split(x)
    out = jnp.dot(high, vhi[...], preferred_element_type=F32)
    out += jnp.dot(low, vhi[...], preferred_element_type=F32)
    out += jnp.dot(high, vlo[...], preferred_element_type=F32)
    return out


def kernel(
    regions, ctl, pert, assign, cour, innov, weight, vhi_in, vlo_in, coef_in,
    lft, dep_out,
    vhi, vlo, coef, ctl3, pbuf, sums, home, smo_out, smo, ms, inc, inc_far, cour_x, inn_x, wgt_x, adj, dep,
    modes, rows, mid, fin,
    load_sem, pert_send, pert_recv, z_send, z_recv, nb_send, nb_recv, pair_send, pair_recv,
    smo_send, smo_recv, fin_send, fin_recv, out_sem,
):
    r, me = lax.axis_index("region"), lax.axis_index("member")
    fl, levels, height, columns = ctl.shape
    kl = pert.shape[0]
    xs = levels // 2
    part_fields = fl * xs
    groups = 2 * part_fields // GROUP
    tiles = columns // 128
    last = regions - 1
    mx, mz = lax.rem(me, xs), me // xs
    beside = [x for x in BESIDE if x < xs]

    def at_x(x):
        return lax.rem(mx + x, xs)

    def beside_me(x):
        return mz * xs + at_x(x)

    across = (1 - mz) * xs + mx

    barrier = pltpu.get_barrier_semaphore()
    for x in beside:
        pl.semaphore_signal(barrier, inc=1, device_id=(r, beside_me(x)), device_id_type=MESH)
    pl.semaphore_signal(barrier, inc=1, device_id=(r, across), device_id_type=MESH)

    @pl.when(r > 0)
    def _():
        for to in (me, across):
            pl.semaphore_signal(barrier, inc=1, device_id=(r - 1, to), device_id_type=MESH)

    @pl.when(r < last)
    def _():
        for to in (me, across):
            pl.semaphore_signal(barrier, inc=1, device_id=(r + 1, to), device_id_type=MESH)

    loads = [
        pltpu.make_async_copy(vhi_in, vhi, load_sem.at[0]),
        pltpu.make_async_copy(vlo_in, vlo, load_sem.at[1]),
        pltpu.make_async_copy(coef_in, coef, load_sem.at[2]),
        pltpu.make_async_copy(ctl, ctl3.at[1], load_sem.at[3]),
        pltpu.make_async_copy(pert.at[:, mx], pbuf.at[0, pl.ds(mx * kl, kl)], load_sem.at[4]),
        pltpu.make_async_copy(pert.at[:, xs + mx], pbuf.at[1, pl.ds(mx * kl, kl)], load_sem.at[5]),
        pltpu.make_async_copy(cour.at[:, :, 0], cour_x.at[:, :, pl.ds(HALO, height)], load_sem.at[6]),
        pltpu.make_async_copy(innov.at[0], inn_x.at[pl.ds(HALO, height)], load_sem.at[7]),
        pltpu.make_async_copy(weight.at[0], wgt_x.at[pl.ds(HALO, height)], load_sem.at[8]),
    ]
    for copy in loads:
        copy.start()

    top, bottom = pl.ds(0, HALO), pl.ds(height - HALO, HALO)
    above, below = pl.ds(0, HALO), pl.ds(HALO + height, HALO)
    halves = (top, bottom)
    nb = [
        ((ctl, ctl3.at[0]), (ctl, ctl3.at[2]), me),
        ((cour.at[:, :, 0, bottom], cour_x.at[:, :, above]), (cour.at[:, :, 0, top], cour_x.at[:, :, below]), me),
        ((innov.at[0, bottom], inn_x.at[above]), (innov.at[0, top], inn_x.at[below]), me),
        ((weight.at[0, bottom], wgt_x.at[above]), (weight.at[0, top], wgt_x.at[below]), me),
        ((ms.at[1, :, :, top], ms.at[0, :, :, top]), (ms.at[1, :, :, top], ms.at[2, :, :, top]), me),
        ((ms.at[1, :, :, bottom], ms.at[0, :, :, bottom]), (ms.at[1, :, :, bottom], ms.at[2, :, :, bottom]), me),
        ((inc.at[0, pl.ds(height, HALO)], inc.at[0, above]), (inc.at[0, pl.ds(HALO, HALO)], inc.at[0, below]), me),
        ((inc_far.at[bottom], inc.at[1, above]), (inc_far.at[top], inc.at[1, below]), across),
        ((adj.at[mz, 1], adj.at[mz, 0]), (adj.at[mz, 1], adj.at[mz, 2]), me),
        ((adj.at[mz, 1], adj.at[mz, 0]), (adj.at[mz, 1], adj.at[mz, 2]), across),
    ]

    def to_neighbour(number, up):
        src, dst = nb[number][up]
        return pltpu.make_async_remote_copy(
            src_ref=src, dst_ref=dst, send_sem=nb_send.at[number, up], recv_sem=nb_recv.at[number, up],
            device_id=(r - 1 if up else r + 1, nb[number][2]), device_id_type=MESH,
        )

    def exchange(number):
        @pl.when(r < last)
        def _():
            to_neighbour(number, 0).start()

        @pl.when(r > 0)
        def _():
            to_neighbour(number, 1).start()

    def arrived(number):
        @pl.when(r > 0)
        def _():
            to_neighbour(number, 0).wait_recv()

        @pl.when(r < last)
        def _():
            to_neighbour(number, 1).wait_recv()

    def sent(number):
        @pl.when(r < last)
        def _():
            to_neighbour(number, 0).wait_send()

        @pl.when(r > 0)
        def _():
            to_neighbour(number, 1).wait_send()

    def pair_copy(number):
        src, dst = ((inc_far, inc.at[1, pl.ds(HALO, height)]), (adj.at[mz, 1], adj.at[mz, 1]))[number]
        return pltpu.make_async_remote_copy(
            src_ref=src, dst_ref=dst, send_sem=pair_send.at[number], recv_sem=pair_recv.at[number],
            device_id=(r, across), device_id_type=MESH,
        )

    def pert_copy(x, z, half):
        return pltpu.make_async_remote_copy(
            src_ref=pert.at[:, z * xs + at_x(x), halves[half]], dst_ref=pbuf.at[z, pl.ds(mx * kl, kl), halves[half]],
            send_sem=pert_send.at[x, z, half], recv_sem=pert_recv.at[x, z, half],
            device_id=(r, beside_me(x)), device_id_type=MESH,
        )

    def z_copy(z, half):
        return pltpu.make_async_remote_copy(
            src_ref=sums.at[z, pl.ds((1 - mz) * part_fields, part_fields), halves[half]],
            dst_ref=home.at[z, :, halves[half]],
            send_sem=z_send.at[z, half], recv_sem=z_recv.at[z, half],
            device_id=(r, across), device_id_type=MESH,
        )

    def smo_copy(x, field):
        return pltpu.make_async_remote_copy(
            src_ref=smo_out.at[field, :, at_x(x)], dst_ref=smo.at[:, mx * fl + field],
            send_sem=smo_send.at[x, field], recv_sem=smo_recv.at[x, field],
            device_id=(r, beside_me(x)), device_id_type=MESH,
        )

    def smo_own(field):
        return pltpu.make_async_copy(smo_out.at[field, :, mx], smo.at[:, mx * fl + field], smo_send.at[0, field])

    def fin_copy(x, z):
        return pltpu.make_async_remote_copy(
            src_ref=fin.at[x, z], dst_ref=lft.at[:, z * xs + mx],
            send_sem=fin_send.at[x, z], recv_sem=fin_recv.at[x, z],
            device_id=(r, beside_me(x)), device_id_type=MESH,
        )

    def fin_own(z):
        return pltpu.make_async_copy(fin.at[0, z], lft.at[:, z * xs + mx], fin_send.at[0, z])

    neighbours = (r > 0).astype(jnp.int32) + (r < last).astype(jnp.int32)
    pl.semaphore_wait(barrier, len(beside) + 1 + 2 * neighbours)

    exchange(0)
    pieces = [(z, half) for half in range(2) for z in range(2)]
    for z, half in pieces:
        for x in beside:
            pert_copy(x, z, half).start()
    for number in (1, 2, 3):
        exchange(number)

    @pl.when(r == 0)
    def _():
        for ref in (inn_x, wgt_x, inc.at[0], inc.at[1]):
            ref[0:HALO] = jnp.zeros((HALO, columns), F32)
        cour_x[:, :, 0:HALO] = jnp.zeros((STEPS, 4, HALO, columns), F32)

    @pl.when(r == last)
    def _():
        for ref in (inn_x, wgt_x, inc.at[0], inc.at[1]):
            ref[HALO + height :] = jnp.zeros((HALO, columns), F32)
        cour_x[:, :, HALO + height :] = jnp.zeros((STEPS, 4, HALO, columns), F32)

    def smooth(x):
        flat = jnp.concatenate([part.reshape(GROUP * height, columns) for part in x], axis=0)
        spectrum = times_sine(flat, vhi, vlo)
        for t in range(tiles):
            lane = slice(t * 128, (t + 1) * 128)
            modes[t] = spectrum[:, lane]
            for part in range(3):
                for i in range(height):
                    rows[part * height + i, :, lane] = modes[t, pl.ds(part * GROUP * height + i, GROUP, stride=height), :]

        @pl.when(r == 0)
        def _():
            rows[height - 1] = jnp.zeros((GROUP, columns), F32)
            for k in range(1, height):
                rows[height - 1 - k] = -rows[height - 1 + k]

        @pl.when(r == last)
        def _():
            rows[2 * height] = jnp.zeros((GROUP, columns), F32)
            for k in range(1, height):
                rows[2 * height + k] = -rows[2 * height - k]

        step = 4

        @pl.loop(0, tiles * (height // step))
        def _(it):
            t = lax.rem(it, tiles)
            lane = pl.ds(pl.multiple_of(t * 128, 128), 128)
            i = (it // tiles) * step
            g = [rows[i + j, :, lane] for j in range(2 * PASSES + step)]
            total = [None] * step
            for d in range(PASSES + 1):
                c = coef[d, :, lane]
                for j in range(step):
                    at = PASSES + j
                    term = c * g[at] if d == 0 else c * (g[at - d] + g[at + d])
                    total[j] = term if d == 0 else total[j] + term
            for j in range(step):
                mid[t, pl.ds(i + j, GROUP, stride=height), :] = total[j]

        result = times_sine(jnp.concatenate([mid[t] for t in range(tiles)], axis=1), vhi, vlo)
        return result.reshape(GROUP, height, columns)

    def add_source(x, z, half, first):
        which = [assign[(mz * xs + x) * kl + k] for k in range(kl)]
        p = [pbuf[z, x * kl + k, halves[half]] for k in range(kl)]
        for l in range(2 * part_fields):
            terms = [jnp.where(which[k] == l, 1.0, 0.0) * p[k] for k in range(kl)]
            while len(terms) > 1:
                terms = [a + b for a, b in zip(terms[::2], terms[1::2])]
            sums[z, l, halves[half]] = terms[0] if first else sums[z, l, halves[half]] + terms[0]

    def add_others(z, half):
        for x in beside:
            pert_copy(x, z, half).wait_recv()
            add_source(at_x(xs - x), z, half, False)
        z_copy(z, half).start()

    def finish(half):
        for z in range(2):
            z_copy(z, half).wait_recv()
            for l in range(part_fields):
                ms[1, z, l, halves[half]] = sums[z, mz * part_fields + l, halves[half]] + home[z, l, halves[half]]
        exchange(4 + half)

    loads[4].wait()
    loads[5].wait()
    for z, half in pieces:
        add_source(mx, z, half, True)
    for z, half in pieces[:2]:
        add_others(z, half)

    for number in range(4):
        loads[number].wait()
    arrived(0)
    for q in range(groups):
        planes = [((q * GROUP + j) // levels, (q * GROUP + j) % levels) for j in range(GROUP)]
        result = smooth([
            jnp.concatenate([ctl3[part, field, level][None] for field, level in planes]) for part in range(3)
        ])
        for j, (field, level) in enumerate(planes):
            smo_out[field, level // xs, level % xs] = result[j]
        for field in range(q * GROUP // levels, (q + 1) * GROUP // levels):
            for x in beside:
                smo_copy(x, field).start()
            smo_own(field).start()

    finish(0)
    for z, half in pieces[2:]:
        add_others(z, half)
    finish(1)

    for field in range(fl):
        smo_own(field).wait()
        for x in beside:
            smo_copy(x, field).wait_recv()

    def share(z):
        total = smo[z, 0] * ms[1, z, 0]
        for l in range(1, part_fields):
            total += smo[z, l] * ms[1, z, l]
        return total

    inc_far[...] = share(1 - mz)
    pair_copy(0).start()
    exchange(7)
    inc[0, HALO : HALO + height] = share(mz)
    exchange(6)
    for number in (6, 7, 8):
        loads[number].wait()
    for number in (1, 2, 3, 6, 7):
        arrived(number)
    pair_copy(0).wait_recv()

    extent = height + 2 * HALO
    column = lax.broadcasted_iota(jnp.int32, (extent, columns), 1)

    def from_west(y):
        return jnp.where(column == 0, 0.0, pltpu.roll(y, 1, 1))

    def from_east(y):
        return jnp.where(column == columns - 1, 0.0, pltpu.roll(y, columns - 1, 1))

    def from_north(y):
        return pltpu.roll(y, 1, 0)

    def from_south(y):
        return pltpu.roll(y, extent - 1, 0)

    state = inc[0] + inc[1]
    for s in range(STEPS):
        n, so, w, e = (cour_x[s, k] for k in range(4))
        state = (
            (1.0 - (n + so + w + e)) * state
            + n * from_north(state) + so * from_south(state) + w * from_west(state) + e * from_east(state)
        )
    state = wgt_x[...] * (state - inn_x[...])
    dep[...] = state[HALO : HALO + height]
    for s in range(STEPS - 1, -1, -1):
        n, so, w, e = (cour_x[s, k] for k in range(4))
        state = (
            (1.0 - (n + so + w + e)) * state
            + from_south(n * state) + from_north(so * state) + from_east(w * state) + from_west(e * state)
        )
    adj[mz, 1] = state[HALO : HALO + height]
    exchange(9)
    exchange(8)
    pair_copy(1).start()
    dep_copy = pltpu.make_async_copy(dep, dep_out.at[0], out_sem)
    dep_copy.start()

    def adj_arrived(up):
        far = 1 - mz
        return pltpu.make_async_remote_copy(
            src_ref=adj.at[far, 1], dst_ref=adj.at[far, 2 if up else 0],
            send_sem=nb_send.at[9, up], recv_sem=nb_recv.at[9, up],
            device_id=(r - 1 if up else r + 1, across), device_id_type=MESH,
        )

    for number in (4, 5, 8):
        arrived(number)

    @pl.when(r > 0)
    def _():
        adj_arrived(0).wait_recv()

    @pl.when(r < last)
    def _():
        adj_arrived(1).wait_recv()

    pltpu.make_async_remote_copy(
        src_ref=adj.at[1 - mz, 1], dst_ref=adj.at[1 - mz, 1], send_sem=pair_send.at[1], recv_sem=pair_recv.at[1],
        device_id=(r, across), device_id_type=MESH,
    ).wait_recv()

    owners = [x for x in (2, 1, 3, 0) if x < xs]
    per = GROUP // (2 * fl)
    for q in range(groups):
        mine = owners[q * per : (q + 1) * per]
        planes = [(x, z, f) for x in mine for z in range(2) for f in range(fl)]
        result = smooth([
            jnp.concatenate([(ms[part, z, at_x(x) * fl + f] * adj[z, part])[None] for x, z, f in planes])
            for part in range(3)
        ])
        for j, (x, z, f) in enumerate(planes):
            fin[x, z, f] = result[j]
        for x in mine:
            for z in range(2):
                if x:
                    fin_copy(x, z).start()
                else:
                    fin_own(z).start()

    for z, half in pieces:
        for x in beside:
            pert_copy(x, z, half).wait_send()
        z_copy(z, half).wait_send()
    for x in beside:
        for field in range(fl):
            smo_copy(x, field).wait_send()
    for number in range(len(nb)):
        sent(number)
    for number in range(2):
        pair_copy(number).wait_send()
    dep_copy.wait()
    for z in range(2):
        fin_own(z).wait()
        for x in beside:
            fin_copy(x, z).wait_send()
    for z in range(2):
        for x in beside:
            fin_copy(x, z).wait_recv()


def solution(mesh):
    regions = mesh.shape["region"]

    def shards(controls, perturbations, assignment, courant, innovation, obs_weight):
        fl, levels, height, columns = controls.shape
        kl = perturbations.shape[0]
        fields, xs = fl * levels, levels // 2
        vhi, vlo, coef = tables(columns)
        extent = height + 2 * HALO
        any_space = pl.BlockSpec(memory_space=pltpu.HBM)
        smem = pl.BlockSpec(memory_space=pltpu.SMEM)
        dma = pltpu.SemaphoreType.DMA
        lft, departure = pl.pallas_call(
            functools.partial(kernel, regions),
            out_shape=(
                jax.ShapeDtypeStruct(controls.shape, F32),
                jax.ShapeDtypeStruct(innovation.shape, F32),
            ),
            in_specs=[any_space, any_space, smem] + [any_space] * 6,
            out_specs=(any_space, any_space),
            scratch_shapes=[
                pltpu.VMEM((columns, columns), BF16),
                pltpu.VMEM((columns, columns), BF16),
                pltpu.VMEM((PASSES + 1, GROUP, columns), F32),
                pltpu.VMEM((3, fl, levels, height, columns), F32),
                pltpu.VMEM((2, kl * xs, height, columns), F32),
                pltpu.VMEM((2, fields, height, columns), F32),
                pltpu.VMEM((2, fl * xs, height, columns), F32),
                pltpu.VMEM((fl, 2, xs, height, columns), F32),
                pltpu.VMEM((2, fl * xs, height, columns), F32),
                pltpu.VMEM((3, 2, fl * xs, height, columns), F32),
                pltpu.VMEM((2, extent, columns), F32),
                pltpu.VMEM((height, columns), F32),
                pltpu.VMEM((STEPS, 4, extent, columns), F32),
                pltpu.VMEM((extent, columns), F32),
                pltpu.VMEM((extent, columns), F32),
                pltpu.VMEM((2, 3, height, columns), F32),
                pltpu.VMEM((height, columns), F32),
                pltpu.VMEM((columns // 128, 3 * GROUP * height, 128), F32),
                pltpu.VMEM((3 * height, GROUP, columns), F32),
                pltpu.VMEM((columns // 128, GROUP * height, 128), F32),
                pltpu.VMEM((xs, 2, fl, height, columns), F32),
                dma((9,)),
                dma((4, 2, 2)),
                dma((4, 2, 2)),
                dma((2, 2)),
                dma((2, 2)),
                dma((10, 2)),
                dma((10, 2)),
                dma((2,)),
                dma((2,)),
                dma((4, fl)),
                dma((4, fl)),
                dma((4, 2)),
                dma((4, 2)),
                dma,
            ],
            compiler_params=pltpu.CompilerParams(
                collective_id=0, has_side_effects=True, vmem_limit_bytes=56 * 2**20
            ),
            cost_estimate=pl.CostEstimate(flops=2 * 10**9, bytes_accessed=8 * 2**20, transcendentals=0),
        )(controls, perturbations, assignment, courant, innovation, obs_weight, vhi, vlo, coef)
        return controls + lft, departure

    return jax.shard_map(
        shards,
        mesh=mesh,
        in_specs=(
            P("member", None, "region", None),
            P("member", None, "region", None),
            P(),
            P(None, None, "member", "region", None),
            P("member", "region", None),
            P("member", "region", None),
        ),
        out_specs=(P("member", None, "region", None), P("member", "region", None)),
        check_vma=False,
    )
```

```python
import functools

import jax
import jax.numpy as jnp
import numpy as np
from jax import lax
from jax.experimental import pallas as pl
from jax.experimental.pallas import tpu as pltpu
from jax.sharding import PartitionSpec as P

PASSES = 16
STEPS = 4
GROUP = 8
HALO = 8
MESH = pl.DeviceIdType.MESH
BESIDE = (1, 3, 2)
F32 = jnp.float32
BF16 = jnp.bfloat16


def tables(columns):
    index = np.arange(1, columns + 1, dtype=np.float64)
    sine = np.sqrt(2.0 / (columns + 1)) * np.sin(np.pi * np.outer(index, index) / (columns + 1))
    high = sine.astype(BF16)
    low = (sine - high.astype(np.float64)).astype(BF16)
    center = (1.0 + 2.0 * np.cos(np.pi * index / (columns + 1))) / 5.0
    power = np.ones((1, columns))
    for _ in range(PASSES):
        wider = np.zeros((power.shape[0] + 2, columns))
        wider[1:-1] += center * power
        wider[2:] += power / 5.0
        wider[:-2] += power / 5.0
        power = wider
    coef = np.broadcast_to(power[PASSES:, None, :], (PASSES + 1, GROUP, columns))
    return high, low, np.ascontiguousarray(coef).astype(np.float32)


def split(x):
    high = x.astype(BF16)
    return high, (x - high.astype(F32)).astype(BF16)


def times_sine(x, vhi, vlo):
    high, low = split(x)
    out = jnp.dot(high, vhi[...], preferred_element_type=F32)
    out += jnp.dot(low, vhi[...], preferred_element_type=F32)
    out += jnp.dot(high, vlo[...], preferred_element_type=F32)
    return out


def kernel(
    regions, ctl, pert, assign, cour, innov, weight, vhi_in, vlo_in, coef_in,
    lft, dep_out,
    vhi, vlo, coef, ctl3, pbuf, sums, home, smo_out, smo, ms, inc, inc_far, cour_x, inn_x, wgt_x, adj, dep,
    modes, rows, mid, fin,
    load_sem, pert_send, pert_recv, z_send, z_recv, nb_send, nb_recv, pair_send, pair_recv,
    smo_send, smo_recv, fin_send, fin_recv, out_sem,
):
    r, me = lax.axis_index("region"), lax.axis_index("member")
    fl, levels, height, columns = ctl.shape
    kl = pert.shape[0]
    xs = levels // 2
    part_fields = fl * xs
    groups = 2 * part_fields // GROUP
    tiles = columns // 128
    last = regions - 1
    mx, mz = lax.rem(me, xs), me // xs
    beside = [x for x in BESIDE if x < xs]

    def at_x(x):
        return lax.rem(mx + x, xs)

    def beside_me(x):
        return mz * xs + at_x(x)

    across = (1 - mz) * xs + mx

    barrier = pltpu.get_barrier_semaphore()
    for x in beside:
        pl.semaphore_signal(barrier, inc=1, device_id=(r, beside_me(x)), device_id_type=MESH)
    pl.semaphore_signal(barrier, inc=1, device_id=(r, across), device_id_type=MESH)

    @pl.when(r > 0)
    def _():
        for to in (me, across):
            pl.semaphore_signal(barrier, inc=1, device_id=(r - 1, to), device_id_type=MESH)

    @pl.when(r < last)
    def _():
        for to in (me, across):
            pl.semaphore_signal(barrier, inc=1, device_id=(r + 1, to), device_id_type=MESH)

    loads = [
        pltpu.make_async_copy(vhi_in, vhi, load_sem.at[0]),
        pltpu.make_async_copy(vlo_in, vlo, load_sem.at[1]),
        pltpu.make_async_copy(coef_in, coef, load_sem.at[2]),
        pltpu.make_async_copy(ctl, ctl3.at[1], load_sem.at[3]),
        pltpu.make_async_copy(pert.at[:, mx], pbuf.at[0, pl.ds(mx * kl, kl)], load_sem.at[4]),
        pltpu.make_async_copy(pert.at[:, xs + mx], pbuf.at[1, pl.ds(mx * kl, kl)], load_sem.at[5]),
        pltpu.make_async_copy(cour.at[:, :, 0], cour_x.at[:, :, pl.ds(HALO, height)], load_sem.at[6]),
        pltpu.make_async_copy(innov.at[0], inn_x.at[pl.ds(HALO, height)], load_sem.at[7]),
        pltpu.make_async_copy(weight.at[0], wgt_x.at[pl.ds(HALO, height)], load_sem.at[8]),
    ]
    for copy in loads:
        copy.start()

    top, bottom = pl.ds(0, HALO), pl.ds(height - HALO, HALO)
    above, below = pl.ds(0, HALO), pl.ds(HALO + height, HALO)
    halves = (top, bottom)
    nb = [
        ((ctl, ctl3.at[0]), (ctl, ctl3.at[2]), me),
        ((cour.at[:, :, 0, bottom], cour_x.at[:, :, above]), (cour.at[:, :, 0, top], cour_x.at[:, :, below]), me),
        ((innov.at[0, bottom], inn_x.at[above]), (innov.at[0, top], inn_x.at[below]), me),
        ((weight.at[0, bottom], wgt_x.at[above]), (weight.at[0, top], wgt_x.at[below]), me),
        ((inc.at[0, pl.ds(height, HALO)], inc.at[0, above]), (inc.at[0, pl.ds(HALO, HALO)], inc.at[0, below]), me),
        ((inc_far.at[bottom], inc.at[1, above]), (inc_far.at[top], inc.at[1, below]), across),
        ((adj.at[mz, 1], adj.at[mz, 0]), (adj.at[mz, 1], adj.at[mz, 2]), me),
        ((adj.at[mz, 1], adj.at[mz, 0]), (adj.at[mz, 1], adj.at[mz, 2]), across),
    ]
    pieces = [(z, half) for half in range(2) for z in range(2)]
    first_piece = len(nb)
    for z, half in pieces:
        own = ms.at[1, z, :, halves[half]]
        nb.append(((own, ms.at[0, z, :, halves[half]]), (own, ms.at[2, z, :, halves[half]]), me))

    def to_neighbour(number, up):
        src, dst = nb[number][up]
        return pltpu.make_async_remote_copy(
            src_ref=src, dst_ref=dst, send_sem=nb_send.at[number, up], recv_sem=nb_recv.at[number, up],
            device_id=(r - 1 if up else r + 1, nb[number][2]), device_id_type=MESH,
        )

    def exchange(number):
        @pl.when(r < last)
        def _():
            to_neighbour(number, 0).start()

        @pl.when(r > 0)
        def _():
            to_neighbour(number, 1).start()

    def arrived(number):
        @pl.when(r > 0)
        def _():
            to_neighbour(number, 0).wait_recv()

        @pl.when(r < last)
        def _():
            to_neighbour(number, 1).wait_recv()

    def sent(number):
        @pl.when(r < last)
        def _():
            to_neighbour(number, 0).wait_send()

        @pl.when(r > 0)
        def _():
            to_neighbour(number, 1).wait_send()

    def pair_copy(number):
        src, dst = ((inc_far, inc.at[1, pl.ds(HALO, height)]), (adj.at[mz, 1], adj.at[mz, 1]))[number]
        return pltpu.make_async_remote_copy(
            src_ref=src, dst_ref=dst, send_sem=pair_send.at[number], recv_sem=pair_recv.at[number],
            device_id=(r, across), device_id_type=MESH,
        )

    def pert_copy(x, z, half):
        return pltpu.make_async_remote_copy(
            src_ref=pert.at[:, z * xs + at_x(x), halves[half]], dst_ref=pbuf.at[z, pl.ds(mx * kl, kl), halves[half]],
            send_sem=pert_send.at[x, z, half], recv_sem=pert_recv.at[x, z, half],
            device_id=(r, beside_me(x)), device_id_type=MESH,
        )

    def z_copy(z, half):
        return pltpu.make_async_remote_copy(
            src_ref=sums.at[z, pl.ds((1 - mz) * part_fields, part_fields), halves[half]],
            dst_ref=home.at[z, :, halves[half]],
            send_sem=z_send.at[z, half], recv_sem=z_recv.at[z, half],
            device_id=(r, across), device_id_type=MESH,
        )

    def smo_copy(x, field):
        return pltpu.make_async_remote_copy(
            src_ref=smo_out.at[field, :, at_x(x)], dst_ref=smo.at[:, mx * fl + field],
            send_sem=smo_send.at[x, field], recv_sem=smo_recv.at[x, field],
            device_id=(r, beside_me(x)), device_id_type=MESH,
        )

    def smo_own(field):
        return pltpu.make_async_copy(smo_out.at[field, :, mx], smo.at[:, mx * fl + field], smo_send.at[0, field])

    def fin_copy(x, z):
        return pltpu.make_async_remote_copy(
            src_ref=fin.at[x, z], dst_ref=lft.at[:, z * xs + mx],
            send_sem=fin_send.at[x, z], recv_sem=fin_recv.at[x, z],
            device_id=(r, beside_me(x)), device_id_type=MESH,
        )

    def fin_own(z):
        return pltpu.make_async_copy(fin.at[0, z], lft.at[:, z * xs + mx], fin_send.at[0, z])

    neighbours = (r > 0).astype(jnp.int32) + (r < last).astype(jnp.int32)
    pl.semaphore_wait(barrier, len(beside) + 1 + 2 * neighbours)

    exchange(0)
    for z, half in pieces:
        for x in beside:
            pert_copy(x, z, half).start()
    for number in (1, 2, 3):
        exchange(number)

    @pl.when(r == 0)
    def _():
        for ref in (inn_x, wgt_x, inc.at[0], inc.at[1]):
            ref[0:HALO] = jnp.zeros((HALO, columns), F32)
        cour_x[:, :, 0:HALO] = jnp.zeros((STEPS, 4, HALO, columns), F32)

    @pl.when(r == last)
    def _():
        for ref in (inn_x, wgt_x, inc.at[0], inc.at[1]):
            ref[HALO + height :] = jnp.zeros((HALO, columns), F32)
        cour_x[:, :, HALO + height :] = jnp.zeros((STEPS, 4, HALO, columns), F32)

    def smooth(x):
        group = x[0].shape[0]
        flat = jnp.concatenate([part.reshape(group * height, columns) for part in x], axis=0)
        spectrum = times_sine(flat, vhi, vlo)
        for t in range(tiles):
            lane = slice(t * 128, (t + 1) * 128)
            modes[t, : 3 * group * height] = spectrum[:, lane]
            for part in range(3):
                for i in range(height):
                    rows[part * height + i, :group, lane] = modes[t, pl.ds(part * group * height + i, group, stride=height), :]

        @pl.when(r == 0)
        def _():
            rows[height - 1] = jnp.zeros((GROUP, columns), F32)
            for k in range(1, height):
                rows[height - 1 - k] = -rows[height - 1 + k]

        @pl.when(r == last)
        def _():
            rows[2 * height] = jnp.zeros((GROUP, columns), F32)
            for k in range(1, height):
                rows[2 * height + k] = -rows[2 * height - k]

        step = 8

        @pl.loop(0, tiles * (height // step))
        def _(it):
            t = lax.rem(it, tiles)
            lane = pl.ds(pl.multiple_of(t * 128, 128), 128)
            i = (it // tiles) * step
            g = [rows[i + j, :group, lane] for j in range(2 * PASSES + step)]
            total = [None] * step
            for d in range(PASSES + 1):
                c = coef[d, :group, lane]
                for j in range(step):
                    at = PASSES + j
                    term = c * g[at] if d == 0 else c * (g[at - d] + g[at + d])
                    total[j] = term if d == 0 else total[j] + term
            for j in range(step):
                mid[t, pl.ds(i + j, group, stride=height), :] = total[j]

        own = jnp.concatenate([mid[t, : group * height] for t in range(tiles)], axis=1)
        return times_sine(own, vhi, vlo).reshape(group, height, columns)

    def add_source(x, z, half, first):
        which = [assign[(mz * xs + x) * kl + k] for k in range(kl)]
        p = [pbuf[z, x * kl + k, halves[half]] for k in range(kl)]
        for l in range(2 * part_fields):
            terms = [jnp.where(which[k] == l, 1.0, 0.0) * p[k] for k in range(kl)]
            while len(terms) > 1:
                terms = [a + b for a, b in zip(terms[::2], terms[1::2])]
            sums[z, l, halves[half]] = terms[0] if first else sums[z, l, halves[half]] + terms[0]

    def add_others(z, half):
        for x in beside:
            pert_copy(x, z, half).wait_recv()
            add_source(at_x(xs - x), z, half, False)
        z_copy(z, half).start()

    def finish(z, half):
        z_copy(z, half).wait_recv()
        for l in range(part_fields):
            ms[1, z, l, halves[half]] = sums[z, mz * part_fields + l, halves[half]] + home[z, l, halves[half]]
        exchange(first_piece + pieces.index((z, half)))

    loads[4].wait()
    loads[5].wait()
    for z, half in pieces:
        add_source(mx, z, half, True)
    for z, half in pieces[:2]:
        add_others(z, half)

    for number in range(4):
        loads[number].wait()
    arrived(0)
    for q in range(groups):
        planes = [((q * GROUP + j) // levels, (q * GROUP + j) % levels) for j in range(GROUP)]
        result = smooth([
            jnp.concatenate([ctl3[part, field, level][None] for field, level in planes]) for part in range(3)
        ])
        for j, (field, level) in enumerate(planes):
            smo_out[field, level // xs, level % xs] = result[j]
        for field in range(q * GROUP // levels, (q + 1) * GROUP // levels):
            for x in beside:
                smo_copy(x, field).start()
            smo_own(field).start()

    for z, half in pieces[:2]:
        finish(z, half)
    for z, half in pieces[2:]:
        add_others(z, half)
    for z, half in pieces[2:]:
        finish(z, half)

    for field in range(fl):
        smo_own(field).wait()
        for x in beside:
            smo_copy(x, field).wait_recv()

    def share(z):
        total = smo[z, 0] * ms[1, z, 0]
        for l in range(1, part_fields):
            total += smo[z, l] * ms[1, z, l]
        return total

    inc_far[...] = share(1 - mz)
    pair_copy(0).start()
    exchange(5)
    inc[0, HALO : HALO + height] = share(mz)
    exchange(4)
    for number in (6, 7, 8):
        loads[number].wait()
    for number in (1, 2, 3, 4, 5):
        arrived(number)
    pair_copy(0).wait_recv()

    extent = height + 2 * HALO
    column = lax.broadcasted_iota(jnp.int32, (extent, columns), 1)

    def from_west(y):
        return jnp.where(column == 0, 0.0, pltpu.roll(y, 1, 1))

    def from_east(y):
        return jnp.where(column == columns - 1, 0.0, pltpu.roll(y, columns - 1, 1))

    def from_north(y):
        return pltpu.roll(y, 1, 0)

    def from_south(y):
        return pltpu.roll(y, extent - 1, 0)

    state = inc[0] + inc[1]
    for s in range(STEPS):
        n, so, w, e = (cour_x[s, k] for k in range(4))
        state = (
            (1.0 - (n + so + w + e)) * state
            + n * from_north(state) + so * from_south(state) + w * from_west(state) + e * from_east(state)
        )
    state = wgt_x[...] * (state - inn_x[...])
    dep[...] = state[HALO : HALO + height]
    for s in range(STEPS - 1, -1, -1):
        n, so, w, e = (cour_x[s, k] for k in range(4))
        state = (
            (1.0 - (n + so + w + e)) * state
            + from_south(n * state) + from_north(so * state) + from_east(w * state) + from_west(e * state)
        )
    adj[mz, 1] = state[HALO : HALO + height]
    exchange(7)
    exchange(6)
    pair_copy(1).start()
    dep_copy = pltpu.make_async_copy(dep, dep_out.at[0], out_sem)
    dep_copy.start()

    def adj_arrived(up):
        far = 1 - mz
        return pltpu.make_async_remote_copy(
            src_ref=adj.at[far, 1], dst_ref=adj.at[far, 2 if up else 0],
            send_sem=nb_send.at[7, up], recv_sem=nb_recv.at[7, up],
            device_id=(r - 1 if up else r + 1, across), device_id_type=MESH,
        )

    for number in [*range(first_piece, len(nb)), 6]:
        arrived(number)

    @pl.when(r > 0)
    def _():
        adj_arrived(0).wait_recv()

    @pl.when(r < last)
    def _():
        adj_arrived(1).wait_recv()

    pltpu.make_async_remote_copy(
        src_ref=adj.at[1 - mz, 1], dst_ref=adj.at[1 - mz, 1], send_sem=pair_send.at[1], recv_sem=pair_recv.at[1],
        device_id=(r, across), device_id_type=MESH,
    ).wait_recv()

    for mine in ((2,), (1, 3), (0,)):
        mine = [x for x in mine if x < xs]
        if not mine:
            continue
        planes = [(x, z, f) for x in mine for z in range(2) for f in range(fl)]
        result = smooth([
            jnp.concatenate([(ms[part, z, at_x(x) * fl + f] * adj[z, part])[None] for x, z, f in planes])
            for part in range(3)
        ])
        for j, (x, z, f) in enumerate(planes):
            fin[x, z, f] = result[j]
        for x in mine:
            for z in range(2):
                if x:
                    fin_copy(x, z).start()
                else:
                    fin_own(z).start()

    for z, half in pieces:
        for x in beside:
            pert_copy(x, z, half).wait_send()
        z_copy(z, half).wait_send()
    for x in beside:
        for field in range(fl):
            smo_copy(x, field).wait_send()
    for number in range(len(nb)):
        sent(number)
    for number in range(2):
        pair_copy(number).wait_send()
    dep_copy.wait()
    for z in range(2):
        fin_own(z).wait()
        for x in beside:
            fin_copy(x, z).wait_send()
    for z in range(2):
        for x in beside:
            fin_copy(x, z).wait_recv()


def solution(mesh):
    regions = mesh.shape["region"]

    def shards(controls, perturbations, assignment, courant, innovation, obs_weight):
        fl, levels, height, columns = controls.shape
        kl = perturbations.shape[0]
        fields, xs = fl * levels, levels // 2
        vhi, vlo, coef = tables(columns)
        extent = height + 2 * HALO
        any_space = pl.BlockSpec(memory_space=pltpu.HBM)
        smem = pl.BlockSpec(memory_space=pltpu.SMEM)
        dma = pltpu.SemaphoreType.DMA
        lft, departure = pl.pallas_call(
            functools.partial(kernel, regions),
            out_shape=(
                jax.ShapeDtypeStruct(controls.shape, F32),
                jax.ShapeDtypeStruct(innovation.shape, F32),
            ),
            in_specs=[any_space, any_space, smem] + [any_space] * 6,
            out_specs=(any_space, any_space),
            scratch_shapes=[
                pltpu.VMEM((columns, columns), BF16),
                pltpu.VMEM((columns, columns), BF16),
                pltpu.VMEM((PASSES + 1, GROUP, columns), F32),
                pltpu.VMEM((3, fl, levels, height, columns), F32),
                pltpu.VMEM((2, kl * xs, height, columns), F32),
                pltpu.VMEM((2, fields, height, columns), F32),
                pltpu.VMEM((2, fl * xs, height, columns), F32),
                pltpu.VMEM((fl, 2, xs, height, columns), F32),
                pltpu.VMEM((2, fl * xs, height, columns), F32),
                pltpu.VMEM((3, 2, fl * xs, height, columns), F32),
                pltpu.VMEM((2, extent, columns), F32),
                pltpu.VMEM((height, columns), F32),
                pltpu.VMEM((STEPS, 4, extent, columns), F32),
                pltpu.VMEM((extent, columns), F32),
                pltpu.VMEM((extent, columns), F32),
                pltpu.VMEM((2, 3, height, columns), F32),
                pltpu.VMEM((height, columns), F32),
                pltpu.VMEM((columns // 128, 3 * GROUP * height, 128), F32),
                pltpu.VMEM((3 * height, GROUP, columns), F32),
                pltpu.VMEM((columns // 128, GROUP * height, 128), F32),
                pltpu.VMEM((xs, 2, fl, height, columns), F32),
                dma((9,)),
                dma((4, 2, 2)),
                dma((4, 2, 2)),
                dma((2, 2)),
                dma((2, 2)),
                dma((12, 2)),
                dma((12, 2)),
                dma((2,)),
                dma((2,)),
                dma((4, fl)),
                dma((4, fl)),
                dma((4, 2)),
                dma((4, 2)),
                dma,
            ],
            compiler_params=pltpu.CompilerParams(
                collective_id=0, has_side_effects=True, vmem_limit_bytes=56 * 2**20
            ),
            cost_estimate=pl.CostEstimate(flops=2 * 10**9, bytes_accessed=8 * 2**20, transcendentals=0),
        )(controls, perturbations, assignment, courant, innovation, obs_weight, vhi, vlo, coef)
        return controls + lft, departure

    return jax.shard_map(
        shards,
        mesh=mesh,
        in_specs=(
            P("member", None, "region", None),
            P("member", None, "region", None),
            P(),
            P(None, None, "member", "region", None),
            P("member", "region", None),
            P("member", "region", None),
        ),
        out_specs=(P("member", None, "region", None), P("member", "region", None)),
        check_vma=False,
    )
```

```python
import functools

import jax
import jax.numpy as jnp
import numpy as np
from jax import lax
from jax.experimental import pallas as pl
from jax.experimental.pallas import tpu as pltpu
from jax.sharding import PartitionSpec as P

PASSES = 16
STEPS = 4
GROUP = 8
HALO = 8
MESH = pl.DeviceIdType.MESH
BESIDE = (1, 3, 2)
F32 = jnp.float32
BF16 = jnp.bfloat16


def tables(columns):
    index = np.arange(1, columns + 1, dtype=np.float64)
    sine = np.sqrt(2.0 / (columns + 1)) * np.sin(np.pi * np.outer(index, index) / (columns + 1))
    high = sine.astype(BF16)
    low = (sine - high.astype(np.float64)).astype(BF16)
    center = (1.0 + 2.0 * np.cos(np.pi * index / (columns + 1))) / 5.0
    power = np.ones((1, columns))
    for _ in range(PASSES):
        wider = np.zeros((power.shape[0] + 2, columns))
        wider[1:-1] += center * power
        wider[2:] += power / 5.0
        wider[:-2] += power / 5.0
        power = wider
    coef = np.broadcast_to(power[PASSES:, None, :], (PASSES + 1, GROUP, columns))
    return high, low, np.ascontiguousarray(coef).astype(np.float32)


def split(x):
    high = x.astype(BF16)
    return high, (x - high.astype(F32)).astype(BF16)


def times_sine(x, vhi, vlo):
    high, low = split(x)
    out = jnp.dot(high, vhi[...], preferred_element_type=F32)
    out += jnp.dot(low, vhi[...], preferred_element_type=F32)
    out += jnp.dot(high, vlo[...], preferred_element_type=F32)
    return out


def kernel(
    regions, ctl, pert, assign, cour, innov, weight, vhi_in, vlo_in, coef_in,
    lft, dep_out,
    vhi, vlo, coef, ctl3, pbuf, sums, home, smo_out, smo, ms, inc, inc_far, cour_x, inn_x, wgt_x, adj, dep,
    modes, rows, mid, fin,
    load_sem, pert_send, pert_recv, z_send, z_recv, nb_send, nb_recv, pair_send, pair_recv,
    smo_send, smo_recv, fin_send, fin_recv, out_sem,
):
    r, me = lax.axis_index("region"), lax.axis_index("member")
    fl, levels, height, columns = ctl.shape
    kl = pert.shape[0]
    xs = levels // 2
    part_fields = fl * xs
    groups = 2 * part_fields // GROUP
    tiles = columns // 128
    last = regions - 1
    mx, mz = lax.rem(me, xs), me // xs
    beside = [x for x in BESIDE if x < xs]

    def at_x(x):
        return lax.rem(mx + x, xs)

    def beside_me(x):
        return mz * xs + at_x(x)

    across = (1 - mz) * xs + mx

    barrier = pltpu.get_barrier_semaphore()
    for x in beside:
        pl.semaphore_signal(barrier, inc=1, device_id=(r, beside_me(x)), device_id_type=MESH)
    pl.semaphore_signal(barrier, inc=1, device_id=(r, across), device_id_type=MESH)

    @pl.when(r > 0)
    def _():
        for to in (me, across):
            pl.semaphore_signal(barrier, inc=1, device_id=(r - 1, to), device_id_type=MESH)

    @pl.when(r < last)
    def _():
        for to in (me, across):
            pl.semaphore_signal(barrier, inc=1, device_id=(r + 1, to), device_id_type=MESH)

    loads = [
        pltpu.make_async_copy(vhi_in, vhi, load_sem.at[0]),
        pltpu.make_async_copy(vlo_in, vlo, load_sem.at[1]),
        pltpu.make_async_copy(coef_in, coef, load_sem.at[2]),
        pltpu.make_async_copy(ctl, ctl3.at[1], load_sem.at[3]),
        pltpu.make_async_copy(pert.at[:, mx], pbuf.at[0, pl.ds(mx * kl, kl)], load_sem.at[4]),
        pltpu.make_async_copy(pert.at[:, xs + mx], pbuf.at[1, pl.ds(mx * kl, kl)], load_sem.at[5]),
        pltpu.make_async_copy(cour.at[:, :, 0], cour_x.at[:, :, pl.ds(HALO, height)], load_sem.at[6]),
        pltpu.make_async_copy(innov.at[0], inn_x.at[pl.ds(HALO, height)], load_sem.at[7]),
        pltpu.make_async_copy(weight.at[0], wgt_x.at[pl.ds(HALO, height)], load_sem.at[8]),
    ]
    for copy in loads:
        copy.start()

    top, bottom = pl.ds(0, HALO), pl.ds(height - HALO, HALO)
    above, below = pl.ds(0, HALO), pl.ds(HALO + height, HALO)
    halves = (top, bottom)
    nb = [
        ((ctl, ctl3.at[0]), (ctl, ctl3.at[2]), me),
        ((cour.at[:, :, 0, bottom], cour_x.at[:, :, above]), (cour.at[:, :, 0, top], cour_x.at[:, :, below]), me),
        ((innov.at[0, bottom], inn_x.at[above]), (innov.at[0, top], inn_x.at[below]), me),
        ((weight.at[0, bottom], wgt_x.at[above]), (weight.at[0, top], wgt_x.at[below]), me),
        ((inc.at[0, pl.ds(height, HALO)], inc.at[0, above]), (inc.at[0, pl.ds(HALO, HALO)], inc.at[0, below]), me),
        ((inc_far.at[bottom], inc.at[1, above]), (inc_far.at[top], inc.at[1, below]), across),
        ((adj.at[mz, 1], adj.at[mz, 0]), (adj.at[mz, 1], adj.at[mz, 2]), me),
        ((adj.at[mz, 1], adj.at[mz, 0]), (adj.at[mz, 1], adj.at[mz, 2]), across),
    ]
    pieces = [(z, half) for half in range(2) for z in range(2)]
    first_piece = len(nb)
    for z, half in pieces:
        own = ms.at[1, z, :, halves[half]]
        nb.append(((own, ms.at[0, z, :, halves[half]]), (own, ms.at[2, z, :, halves[half]]), me))

    def to_neighbour(number, up):
        src, dst = nb[number][up]
        return pltpu.make_async_remote_copy(
            src_ref=src, dst_ref=dst, send_sem=nb_send.at[number, up], recv_sem=nb_recv.at[number, up],
            device_id=(r - 1 if up else r + 1, nb[number][2]), device_id_type=MESH,
        )

    def exchange(number):
        @pl.when(r < last)
        def _():
            to_neighbour(number, 0).start()

        @pl.when(r > 0)
        def _():
            to_neighbour(number, 1).start()

    def arrived(number):
        @pl.when(r > 0)
        def _():
            to_neighbour(number, 0).wait_recv()

        @pl.when(r < last)
        def _():
            to_neighbour(number, 1).wait_recv()

    def sent(number):
        @pl.when(r < last)
        def _():
            to_neighbour(number, 0).wait_send()

        @pl.when(r > 0)
        def _():
            to_neighbour(number, 1).wait_send()

    def pair_copy(number):
        src, dst = ((inc_far, inc.at[1, pl.ds(HALO, height)]), (adj.at[mz, 1], adj.at[mz, 1]))[number]
        return pltpu.make_async_remote_copy(
            src_ref=src, dst_ref=dst, send_sem=pair_send.at[number], recv_sem=pair_recv.at[number],
            device_id=(r, across), device_id_type=MESH,
        )

    def pert_copy(x, z, half):
        return pltpu.make_async_remote_copy(
            src_ref=pert.at[:, z * xs + at_x(x), halves[half]], dst_ref=pbuf.at[z, pl.ds(mx * kl, kl), halves[half]],
            send_sem=pert_send.at[x, z, half], recv_sem=pert_recv.at[x, z, half],
            device_id=(r, beside_me(x)), device_id_type=MESH,
        )

    def z_copy(z, half):
        return pltpu.make_async_remote_copy(
            src_ref=sums.at[z, pl.ds((1 - mz) * part_fields, part_fields), halves[half]],
            dst_ref=home.at[z, :, halves[half]],
            send_sem=z_send.at[z, half], recv_sem=z_recv.at[z, half],
            device_id=(r, across), device_id_type=MESH,
        )

    def smo_copy(x, field):
        return pltpu.make_async_remote_copy(
            src_ref=smo_out.at[field, :, at_x(x)], dst_ref=smo.at[:, mx * fl + field],
            send_sem=smo_send.at[x, field], recv_sem=smo_recv.at[x, field],
            device_id=(r, beside_me(x)), device_id_type=MESH,
        )

    def smo_own(field):
        return pltpu.make_async_copy(smo_out.at[field, :, mx], smo.at[:, mx * fl + field], smo_send.at[0, field])

    def fin_copy(x, z):
        return pltpu.make_async_remote_copy(
            src_ref=fin.at[x, z], dst_ref=lft.at[:, z * xs + mx],
            send_sem=fin_send.at[x, z], recv_sem=fin_recv.at[x, z],
            device_id=(r, beside_me(x)), device_id_type=MESH,
        )

    def fin_own(z):
        return pltpu.make_async_copy(fin.at[0, z], lft.at[:, z * xs + mx], fin_send.at[0, z])

    neighbours = (r > 0).astype(jnp.int32) + (r < last).astype(jnp.int32)
    pl.semaphore_wait(barrier, len(beside) + 1 + 2 * neighbours)

    exchange(0)
    for z, half in pieces:
        for x in beside:
            pert_copy(x, z, half).start()
    for number in (1, 2, 3):
        exchange(number)

    @pl.when(r == 0)
    def _():
        for ref in (inn_x, wgt_x, inc.at[0], inc.at[1]):
            ref[0:HALO] = jnp.zeros((HALO, columns), F32)
        cour_x[:, :, 0:HALO] = jnp.zeros((STEPS, 4, HALO, columns), F32)

    @pl.when(r == last)
    def _():
        for ref in (inn_x, wgt_x, inc.at[0], inc.at[1]):
            ref[HALO + height :] = jnp.zeros((HALO, columns), F32)
        cour_x[:, :, HALO + height :] = jnp.zeros((STEPS, 4, HALO, columns), F32)

    def smooth(x):
        group = x[0].shape[0]
        flat = jnp.concatenate([part.reshape(group * height, columns) for part in x], axis=0)
        spectrum = times_sine(flat, vhi, vlo)
        for t in range(tiles):
            lane = slice(t * 128, (t + 1) * 128)
            modes[t, : 3 * group * height] = spectrum[:, lane]
            for part in range(3):
                for i in range(height):
                    rows[part * height + i, :group, lane] = modes[t, pl.ds(part * group * height + i, group, stride=height), :]

        @pl.when(r == 0)
        def _():
            rows[height - 1] = jnp.zeros((GROUP, columns), F32)
            for k in range(1, height):
                rows[height - 1 - k] = -rows[height - 1 + k]

        @pl.when(r == last)
        def _():
            rows[2 * height] = jnp.zeros((GROUP, columns), F32)
            for k in range(1, height):
                rows[2 * height + k] = -rows[2 * height - k]

        step = 8

        @pl.loop(0, tiles * (height // step))
        def _(it):
            t = lax.rem(it, tiles)
            lane = pl.ds(pl.multiple_of(t * 128, 128), 128)
            i = (it // tiles) * step
            g = [rows[i + j, :group, lane] for j in range(2 * PASSES + step)]
            total = [None] * step
            for d in range(PASSES + 1):
                c = coef[d, :group, lane]
                for j in range(step):
                    at = PASSES + j
                    term = c * g[at] if d == 0 else c * (g[at - d] + g[at + d])
                    total[j] = term if d == 0 else total[j] + term
            for j in range(step):
                mid[t, pl.ds(i + j, group, stride=height), :] = total[j]

        own = jnp.concatenate([mid[t, : group * height] for t in range(tiles)], axis=1)
        return times_sine(own, vhi, vlo).reshape(group, height, columns)

    def add_source(x, z, half, first):
        which = [assign[(mz * xs + x) * kl + k] for k in range(kl)]
        p = [pbuf[z, x * kl + k, halves[half]] for k in range(kl)]
        for l in range(2 * part_fields):
            terms = [jnp.where(which[k] == l, 1.0, 0.0) * p[k] for k in range(kl)]
            while len(terms) > 1:
                terms = [a + b for a, b in zip(terms[::2], terms[1::2])]
            sums[z, l, halves[half]] = terms[0] if first else sums[z, l, halves[half]] + terms[0]

    def add_others(z, half):
        for x in beside:
            pert_copy(x, z, half).wait_recv()
            add_source(at_x(xs - x), z, half, False)
        z_copy(z, half).start()

    def finish(z, half):
        z_copy(z, half).wait_recv()
        for l in range(part_fields):
            ms[1, z, l, halves[half]] = sums[z, mz * part_fields + l, halves[half]] + home[z, l, halves[half]]
        exchange(first_piece + pieces.index((z, half)))

    loads[4].wait()
    loads[5].wait()
    for z, half in pieces:
        add_source(mx, z, half, True)
    for z, half in pieces[:2]:
        add_others(z, half)

    for number in range(4):
        loads[number].wait()
    arrived(0)
    for q in range(groups):
        planes = [((q * GROUP + j) // levels, (q * GROUP + j) % levels) for j in range(GROUP)]
        result = smooth([
            jnp.concatenate([ctl3[part, field, level][None] for field, level in planes]) for part in range(3)
        ])
        for j, (field, level) in enumerate(planes):
            smo_out[field, level // xs, level % xs] = result[j]
        for field in range(q * GROUP // levels, (q + 1) * GROUP // levels):
            for x in beside:
                smo_copy(x, field).start()
            smo_own(field).start()

    for z, half in pieces[:2]:
        finish(z, half)
    for z, half in pieces[2:]:
        add_others(z, half)
    for z, half in pieces[2:]:
        finish(z, half)

    for field in range(fl):
        smo_own(field).wait()
        for x in beside:
            smo_copy(x, field).wait_recv()

    def share(z):
        total = smo[z, 0] * ms[1, z, 0]
        for l in range(1, part_fields):
            total += smo[z, l] * ms[1, z, l]
        return total

    inc_far[...] = share(1 - mz)
    pair_copy(0).start()
    exchange(5)
    inc[0, HALO : HALO + height] = share(mz)
    exchange(4)
    for number in (6, 7, 8):
        loads[number].wait()
    for number in (1, 2, 3, 4, 5):
        arrived(number)
    pair_copy(0).wait_recv()

    extent = height + 2 * HALO
    column = lax.broadcasted_iota(jnp.int32, (extent, columns), 1)

    def from_west(y):
        return jnp.where(column == 0, 0.0, pltpu.roll(y, 1, 1))

    def from_east(y):
        return jnp.where(column == columns - 1, 0.0, pltpu.roll(y, columns - 1, 1))

    def from_north(y):
        return pltpu.roll(y, 1, 0)

    def from_south(y):
        return pltpu.roll(y, extent - 1, 0)

    state = inc[0] + inc[1]
    for s in range(STEPS):
        n, so, w, e = (cour_x[s, k] for k in range(4))
        state = (
            (1.0 - (n + so + w + e)) * state
            + n * from_north(state) + so * from_south(state) + w * from_west(state) + e * from_east(state)
        )
    state = wgt_x[...] * (state - inn_x[...])
    dep[...] = state[HALO : HALO + height]
    for s in range(STEPS - 1, -1, -1):
        n, so, w, e = (cour_x[s, k] for k in range(4))
        state = (
            (1.0 - (n + so + w + e)) * state
            + from_south(n * state) + from_north(so * state) + from_east(w * state) + from_west(e * state)
        )
    adj[mz, 1] = state[HALO : HALO + height]
    exchange(7)
    exchange(6)
    pair_copy(1).start()
    dep_copy = pltpu.make_async_copy(dep, dep_out.at[0], out_sem)
    dep_copy.start()

    def adj_arrived(up):
        far = 1 - mz
        return pltpu.make_async_remote_copy(
            src_ref=adj.at[far, 1], dst_ref=adj.at[far, 2 if up else 0],
            send_sem=nb_send.at[7, up], recv_sem=nb_recv.at[7, up],
            device_id=(r - 1 if up else r + 1, across), device_id_type=MESH,
        )

    for number in [*range(first_piece, len(nb)), 6]:
        arrived(number)

    @pl.when(r > 0)
    def _():
        adj_arrived(0).wait_recv()

    @pl.when(r < last)
    def _():
        adj_arrived(1).wait_recv()

    pltpu.make_async_remote_copy(
        src_ref=adj.at[1 - mz, 1], dst_ref=adj.at[1 - mz, 1], send_sem=pair_send.at[1], recv_sem=pair_recv.at[1],
        device_id=(r, across), device_id_type=MESH,
    ).wait_recv()

    for mine in ((2,), (1, 3), (0,)):
        mine = [x for x in mine if x < xs]
        if not mine:
            continue
        planes = [(x, z, f) for x in mine for z in range(2) for f in range(fl)]
        result = smooth([
            jnp.concatenate([(ms[part, z, at_x(x) * fl + f] * adj[z, part])[None] for x, z, f in planes])
            for part in range(3)
        ])
        for j, (x, z, f) in enumerate(planes):
            fin[x, z, f] = result[j]
        for x in mine:
            for z in range(2):
                if x:
                    fin_copy(x, z).start()
                else:
                    fin_own(z).start()

    for z, half in pieces:
        for x in beside:
            pert_copy(x, z, half).wait_send()
        z_copy(z, half).wait_send()
    for x in beside:
        for field in range(fl):
            smo_copy(x, field).wait_send()
    for number in range(len(nb)):
        sent(number)
    for number in range(2):
        pair_copy(number).wait_send()
    dep_copy.wait()
    for z in range(2):
        fin_own(z).wait()
        for x in beside:
            fin_copy(x, z).wait_send()
    for z in range(2):
        for x in beside:
            fin_copy(x, z).wait_recv()


def solution(mesh):
    regions = mesh.shape["region"]

    def shards(controls, perturbations, assignment, courant, innovation, obs_weight):
        fl, levels, height, columns = controls.shape
        kl = perturbations.shape[0]
        fields, xs = fl * levels, levels // 2
        vhi, vlo, coef = tables(columns)
        extent = height + 2 * HALO
        in_hbm = pl.BlockSpec(memory_space=pltpu.HBM)
        smem = pl.BlockSpec(memory_space=pltpu.SMEM)
        dma = pltpu.SemaphoreType.DMA
        lft, departure = pl.pallas_call(
            functools.partial(kernel, regions),
            out_shape=(
                pltpu.VMEM(controls.shape, F32),
                pltpu.VMEM(innovation.shape, F32),
            ),
            in_specs=[in_hbm, in_hbm, smem] + [in_hbm] * 6,
            out_specs=(pl.BlockSpec(memory_space=pl.ANY),) * 2,
            scratch_shapes=[
                pltpu.VMEM((columns, columns), BF16),
                pltpu.VMEM((columns, columns), BF16),
                pltpu.VMEM((PASSES + 1, GROUP, columns), F32),
                pltpu.VMEM((3, fl, levels, height, columns), F32),
                pltpu.VMEM((2, kl * xs, height, columns), F32),
                pltpu.VMEM((2, fields, height, columns), F32),
                pltpu.VMEM((2, fl * xs, height, columns), F32),
                pltpu.VMEM((fl, 2, xs, height, columns), F32),
                pltpu.VMEM((2, fl * xs, height, columns), F32),
                pltpu.VMEM((3, 2, fl * xs, height, columns), F32),
                pltpu.VMEM((2, extent, columns), F32),
                pltpu.VMEM((height, columns), F32),
                pltpu.VMEM((STEPS, 4, extent, columns), F32),
                pltpu.VMEM((extent, columns), F32),
                pltpu.VMEM((extent, columns), F32),
                pltpu.VMEM((2, 3, height, columns), F32),
                pltpu.VMEM((height, columns), F32),
                pltpu.VMEM((columns // 128, 3 * GROUP * height, 128), F32),
                pltpu.VMEM((3 * height, GROUP, columns), F32),
                pltpu.VMEM((columns // 128, GROUP * height, 128), F32),
                pltpu.VMEM((xs, 2, fl, height, columns), F32),
                dma((9,)),
                dma((4, 2, 2)),
                dma((4, 2, 2)),
                dma((2, 2)),
                dma((2, 2)),
                dma((12, 2)),
                dma((12, 2)),
                dma((2,)),
                dma((2,)),
                dma((4, fl)),
                dma((4, fl)),
                dma((4, 2)),
                dma((4, 2)),
                dma,
            ],
            compiler_params=pltpu.CompilerParams(
                collective_id=0, has_side_effects=True, vmem_limit_bytes=56 * 2**20
            ),
            cost_estimate=pl.CostEstimate(flops=2 * 10**9, bytes_accessed=8 * 2**20, transcendentals=0),
        )(controls, perturbations, assignment, courant, innovation, obs_weight, vhi, vlo, coef)
        return controls + lft, departure

    return jax.shard_map(
        shards,
        mesh=mesh,
        in_specs=(
            P("member", None, "region", None),
            P("member", None, "region", None),
            P(),
            P(None, None, "member", "region", None),
            P("member", "region", None),
            P("member", "region", None),
        ),
        out_specs=(P("member", None, "region", None), P("member", "region", None)),
        check_vma=False,
    )
```

```python
import functools

import jax
import jax.numpy as jnp
import numpy as np
from jax import lax
from jax.experimental import pallas as pl
from jax.experimental.pallas import tpu as pltpu
from jax.sharding import PartitionSpec as P

PASSES = 16
STEPS = 4
GROUP = 8
HALO = 8
MESH = pl.DeviceIdType.MESH
BESIDE = (1, 3, 2)
F32 = jnp.float32
BF16 = jnp.bfloat16


def tables(columns):
    index = np.arange(1, columns + 1, dtype=np.float64)
    sine = np.sqrt(2.0 / (columns + 1)) * np.sin(np.pi * np.outer(index, index) / (columns + 1))
    high = sine.astype(BF16)
    low = (sine - high.astype(np.float64)).astype(BF16)
    center = (1.0 + 2.0 * np.cos(np.pi * index / (columns + 1))) / 5.0
    power = np.ones((1, columns))
    for _ in range(PASSES):
        wider = np.zeros((power.shape[0] + 2, columns))
        wider[1:-1] += center * power
        wider[2:] += power / 5.0
        wider[:-2] += power / 5.0
        power = wider
    coef = np.broadcast_to(power[PASSES:, None, :], (PASSES + 1, GROUP, columns))
    return high, low, np.ascontiguousarray(coef).astype(np.float32)


def split(x):
    high = x.astype(BF16)
    return high, (x - high.astype(F32)).astype(BF16)


def times_sine(x, vhi, vlo):
    high, low = split(x)
    out = jnp.dot(high, vhi[...], preferred_element_type=F32)
    out += jnp.dot(low, vhi[...], preferred_element_type=F32)
    out += jnp.dot(high, vlo[...], preferred_element_type=F32)
    return out


def kernel(
    regions, ctl, pert, assign, cour, innov, weight, vhi_in, vlo_in, coef_in,
    lft, dep_out,
    vhi, vlo, coef, ctl3, pbuf, sums, home, smo_out, smo, ms, inc, inc_far, cour_x, inn_x, wgt_x, adj, dep,
    modes, rows, mid, fin,
    load_sem, pert_send, pert_recv, z_send, z_recv, nb_send, nb_recv, pair_send, pair_recv,
    smo_send, smo_recv, fin_send, fin_recv, out_sem,
):
    r, me = lax.axis_index("region"), lax.axis_index("member")
    fl, levels, height, columns = ctl.shape
    kl = pert.shape[0]
    xs = levels // 2
    part_fields = fl * xs
    groups = 2 * part_fields // GROUP
    tiles = columns // 128
    last = regions - 1
    mx, mz = lax.rem(me, xs), me // xs
    beside = [x for x in BESIDE if x < xs]

    def at_x(x):
        return lax.rem(mx + x, xs)

    def beside_me(x):
        return mz * xs + at_x(x)

    across = (1 - mz) * xs + mx

    barrier = pltpu.get_barrier_semaphore()
    for x in beside:
        pl.semaphore_signal(barrier, inc=1, device_id=(r, beside_me(x)), device_id_type=MESH)
    pl.semaphore_signal(barrier, inc=1, device_id=(r, across), device_id_type=MESH)

    @pl.when(r > 0)
    def _():
        for to in (me, across):
            pl.semaphore_signal(barrier, inc=1, device_id=(r - 1, to), device_id_type=MESH)

    @pl.when(r < last)
    def _():
        for to in (me, across):
            pl.semaphore_signal(barrier, inc=1, device_id=(r + 1, to), device_id_type=MESH)

    loads = [
        pltpu.make_async_copy(vhi_in, vhi, load_sem.at[0]),
        pltpu.make_async_copy(vlo_in, vlo, load_sem.at[1]),
        pltpu.make_async_copy(coef_in, coef, load_sem.at[2]),
        pltpu.make_async_copy(ctl, ctl3.at[1], load_sem.at[3]),
        pltpu.make_async_copy(pert.at[:, mx], pbuf.at[0, pl.ds(mx * kl, kl)], load_sem.at[4]),
        pltpu.make_async_copy(pert.at[:, xs + mx], pbuf.at[1, pl.ds(mx * kl, kl)], load_sem.at[5]),
        pltpu.make_async_copy(cour.at[:, :, 0], cour_x.at[:, :, pl.ds(HALO, height)], load_sem.at[6]),
        pltpu.make_async_copy(innov.at[0], inn_x.at[pl.ds(HALO, height)], load_sem.at[7]),
        pltpu.make_async_copy(weight.at[0], wgt_x.at[pl.ds(HALO, height)], load_sem.at[8]),
    ]
    for copy in loads:
        copy.start()

    top, bottom = pl.ds(0, HALO), pl.ds(height - HALO, HALO)
    above, below = pl.ds(0, HALO), pl.ds(HALO + height, HALO)
    halves = (top, bottom)
    nb = [
        ((ctl, ctl3.at[0]), (ctl, ctl3.at[2]), me),
        ((cour.at[:, :, 0, bottom], cour_x.at[:, :, above]), (cour.at[:, :, 0, top], cour_x.at[:, :, below]), me),
        ((innov.at[0, bottom], inn_x.at[above]), (innov.at[0, top], inn_x.at[below]), me),
        ((weight.at[0, bottom], wgt_x.at[above]), (weight.at[0, top], wgt_x.at[below]), me),
        ((inc.at[0, pl.ds(height, HALO)], inc.at[0, above]), (inc.at[0, pl.ds(HALO, HALO)], inc.at[0, below]), me),
        ((inc_far.at[bottom], inc.at[1, above]), (inc_far.at[top], inc.at[1, below]), across),
        ((adj.at[mz, 1], adj.at[mz, 0]), (adj.at[mz, 1], adj.at[mz, 2]), me),
        ((adj.at[mz, 1], adj.at[mz, 0]), (adj.at[mz, 1], adj.at[mz, 2]), across),
    ]
    pieces = [(z, half) for z in range(2) for half in range(2)]
    first_piece = len(nb)
    for z, half in pieces:
        own = ms.at[1, z, :, halves[half]]
        nb.append(((own, ms.at[0, z, :, halves[half]]), (own, ms.at[2, z, :, halves[half]]), me))

    def to_neighbour(number, up):
        src, dst = nb[number][up]
        return pltpu.make_async_remote_copy(
            src_ref=src, dst_ref=dst, send_sem=nb_send.at[number, up], recv_sem=nb_recv.at[number, up],
            device_id=(r - 1 if up else r + 1, nb[number][2]), device_id_type=MESH,
        )

    def exchange(number):
        @pl.when(r < last)
        def _():
            to_neighbour(number, 0).start()

        @pl.when(r > 0)
        def _():
            to_neighbour(number, 1).start()

    def arrived(number):
        @pl.when(r > 0)
        def _():
            to_neighbour(number, 0).wait_recv()

        @pl.when(r < last)
        def _():
            to_neighbour(number, 1).wait_recv()

    def sent(number):
        @pl.when(r < last)
        def _():
            to_neighbour(number, 0).wait_send()

        @pl.when(r > 0)
        def _():
            to_neighbour(number, 1).wait_send()

    def pair_copy(number):
        src, dst = ((inc_far, inc.at[1, pl.ds(HALO, height)]), (adj.at[mz, 1], adj.at[mz, 1]))[number]
        return pltpu.make_async_remote_copy(
            src_ref=src, dst_ref=dst, send_sem=pair_send.at[number], recv_sem=pair_recv.at[number],
            device_id=(r, across), device_id_type=MESH,
        )

    def pert_copy(x, z, half):
        return pltpu.make_async_remote_copy(
            src_ref=pert.at[:, z * xs + at_x(x), halves[half]], dst_ref=pbuf.at[z, pl.ds(mx * kl, kl), halves[half]],
            send_sem=pert_send.at[x, z, half], recv_sem=pert_recv.at[x, z, half],
            device_id=(r, beside_me(x)), device_id_type=MESH,
        )

    def z_copy(z, half):
        return pltpu.make_async_remote_copy(
            src_ref=sums.at[z, pl.ds((1 - mz) * part_fields, part_fields), halves[half]],
            dst_ref=home.at[z, :, halves[half]],
            send_sem=z_send.at[z, half], recv_sem=z_recv.at[z, half],
            device_id=(r, across), device_id_type=MESH,
        )

    def smo_copy(x, field, z):
        return pltpu.make_async_remote_copy(
            src_ref=smo_out.at[field, z, at_x(x)], dst_ref=smo.at[z, mx * fl + field],
            send_sem=smo_send.at[x, field, z], recv_sem=smo_recv.at[x, field, z],
            device_id=(r, beside_me(x)), device_id_type=MESH,
        )

    def smo_own(field, z):
        return pltpu.make_async_copy(smo_out.at[field, z, mx], smo.at[z, mx * fl + field], smo_send.at[0, field, z])

    def send_smoothed(field, z):
        for x in beside:
            smo_copy(x, field, z).start()
        smo_own(field, z).start()

    def fin_copy(x, z):
        return pltpu.make_async_remote_copy(
            src_ref=fin.at[x, z], dst_ref=lft.at[:, z * xs + mx],
            send_sem=fin_send.at[x, z], recv_sem=fin_recv.at[x, z],
            device_id=(r, beside_me(x)), device_id_type=MESH,
        )

    def fin_own(z):
        return pltpu.make_async_copy(fin.at[0, z], lft.at[:, z * xs + mx], fin_send.at[0, z])

    neighbours = (r > 0).astype(jnp.int32) + (r < last).astype(jnp.int32)
    pl.semaphore_wait(barrier, len(beside) + 1 + 2 * neighbours)

    exchange(0)
    def send_piece(z, half):
        for x in beside:
            pert_copy(x, z, half).start()

    for z, half in pieces[:2]:
        send_piece(z, half)
    for number in (1, 2, 3):
        exchange(number)

    @pl.when(r == 0)
    def _():
        for ref in (inn_x, wgt_x, inc.at[0], inc.at[1]):
            ref[0:HALO] = jnp.zeros((HALO, columns), F32)
        cour_x[:, :, 0:HALO] = jnp.zeros((STEPS, 4, HALO, columns), F32)

    @pl.when(r == last)
    def _():
        for ref in (inn_x, wgt_x, inc.at[0], inc.at[1]):
            ref[HALO + height :] = jnp.zeros((HALO, columns), F32)
        cour_x[:, :, HALO + height :] = jnp.zeros((STEPS, 4, HALO, columns), F32)

    def smooth(x):
        group = x[0].shape[0]
        flat = jnp.concatenate([part.reshape(group * height, columns) for part in x], axis=0)
        spectrum = times_sine(flat, vhi, vlo)
        for t in range(tiles):
            lane = slice(t * 128, (t + 1) * 128)
            modes[t, : 3 * group * height] = spectrum[:, lane]
            for part in range(3):
                for i in range(height):
                    rows[part * height + i, :group, lane] = modes[t, pl.ds(part * group * height + i, group, stride=height), :]

        @pl.when(r == 0)
        def _():
            rows[height - 1] = jnp.zeros((GROUP, columns), F32)
            for k in range(1, height):
                rows[height - 1 - k] = -rows[height - 1 + k]

        @pl.when(r == last)
        def _():
            rows[2 * height] = jnp.zeros((GROUP, columns), F32)
            for k in range(1, height):
                rows[2 * height + k] = -rows[2 * height - k]

        step = 8

        @pl.loop(0, tiles * (height // step))
        def _(it):
            t = lax.rem(it, tiles)
            lane = pl.ds(pl.multiple_of(t * 128, 128), 128)
            i = (it // tiles) * step
            g = [rows[i + j, :group, lane] for j in range(2 * PASSES + step)]
            total = [None] * step
            for d in range(PASSES + 1):
                c = coef[d, :group, lane]
                for j in range(step):
                    at = PASSES + j
                    term = c * g[at] if d == 0 else c * (g[at - d] + g[at + d])
                    total[j] = term if d == 0 else total[j] + term
            for j in range(step):
                mid[t, pl.ds(i + j, group, stride=height), :] = total[j]

        own = jnp.concatenate([mid[t, : group * height] for t in range(tiles)], axis=1)
        return times_sine(own, vhi, vlo).reshape(group, height, columns)

    def add_source(x, z, half, first):
        which = [assign[(mz * xs + x) * kl + k] for k in range(kl)]
        p = [pbuf[z, x * kl + k, halves[half]] for k in range(kl)]
        for l in range(2 * part_fields):
            terms = [jnp.where(which[k] == l, 1.0, 0.0) * p[k] for k in range(kl)]
            while len(terms) > 1:
                terms = [a + b for a, b in zip(terms[::2], terms[1::2])]
            sums[z, l, halves[half]] = terms[0] if first else sums[z, l, halves[half]] + terms[0]

    def add_others(z, half):
        for x in beside:
            pert_copy(x, z, half).wait_recv()
            add_source(at_x(xs - x), z, half, False)
        z_copy(z, half).start()

    def finish(z, half):
        z_copy(z, half).wait_recv()
        for l in range(part_fields):
            ms[1, z, l, halves[half]] = sums[z, mz * part_fields + l, halves[half]] + home[z, l, halves[half]]
        exchange(first_piece + pieces.index((z, half)))

    loads[4].wait()
    loads[5].wait()
    for z, half in pieces:
        add_source(mx, z, half, True)
    add_others(0, 0)
    send_piece(1, 0)

    for number in range(4):
        loads[number].wait()
    arrived(0)
    for q in range(groups):
        planes = [((q * GROUP + j) // levels, (q * GROUP + j) % levels) for j in range(GROUP)]
        result = smooth([
            jnp.concatenate([ctl3[part, field, level][None] for field, level in planes]) for part in range(3)
        ])
        for j, (field, level) in enumerate(planes):
            smo_out[field, level // xs, level % xs] = result[j]
        for field in range(q * GROUP // levels, (q + 1) * GROUP // levels):
            send_smoothed(field, 0)
    send_piece(1, 1)
    for field in range(fl):
        send_smoothed(field, 1)

    def increment(z):
        for field in range(fl):
            smo_own(field, z).wait()
            for x in beside:
                smo_copy(x, field, z).wait_recv()
        total = smo[z, 0] * ms[1, z, 0]
        for l in range(1, part_fields):
            total += smo[z, l] * ms[1, z, l]

        @pl.when(mz == z)
        def _():
            inc[0, HALO : HALO + height] = total
            exchange(4)

        @pl.when(mz != z)
        def _():
            inc_far[...] = total
            pair_copy(0).start()
            exchange(5)

    extent = height + 2 * HALO
    column = lax.broadcasted_iota(jnp.int32, (extent, columns), 1)

    def from_west(y):
        return jnp.where(column == 0, 0.0, pltpu.roll(y, 1, 1))

    def from_east(y):
        return jnp.where(column == columns - 1, 0.0, pltpu.roll(y, columns - 1, 1))

    def from_north(y):
        return pltpu.roll(y, 1, 0)

    def from_south(y):
        return pltpu.roll(y, extent - 1, 0)

    dep_copy = pltpu.make_async_copy(dep, dep_out.at[0], out_sem)

    def transport():
        for number in (6, 7, 8):
            loads[number].wait()
        for number in (1, 2, 3, 4, 5):
            arrived(number)
        pair_copy(0).wait_recv()
        state = inc[0] + inc[1]
        for s in range(STEPS):
            n, so, w, e = (cour_x[s, k] for k in range(4))
            state = (
                (1.0 - (n + so + w + e)) * state
                + n * from_north(state) + so * from_south(state) + w * from_west(state) + e * from_east(state)
            )
        state = wgt_x[...] * (state - inn_x[...])
        dep[...] = state[HALO : HALO + height]
        for s in range(STEPS - 1, -1, -1):
            n, so, w, e = (cour_x[s, k] for k in range(4))
            state = (
                (1.0 - (n + so + w + e)) * state
                + from_south(n * state) + from_north(so * state) + from_east(w * state) + from_west(e * state)
            )
        adj[mz, 1] = state[HALO : HALO + height]
        exchange(7)
        exchange(6)
        pair_copy(1).start()
        dep_copy.start()

    def adj_arrived(up):
        far = 1 - mz
        return pltpu.make_async_remote_copy(
            src_ref=adj.at[far, 1], dst_ref=adj.at[far, 2 if up else 0],
            send_sem=nb_send.at[7, up], recv_sem=nb_recv.at[7, up],
            device_id=(r - 1 if up else r + 1, across), device_id_type=MESH,
        )

    def adj_pair_arrived():
        return pltpu.make_async_remote_copy(
            src_ref=adj.at[1 - mz, 1], dst_ref=adj.at[1 - mz, 1], send_sem=pair_send.at[1], recv_sem=pair_recv.at[1],
            device_id=(r, across), device_id_type=MESH,
        )

    def second(z, chunks):
        for half in range(2):
            arrived(first_piece + pieces.index((z, half)))

        @pl.when(mz == z)
        def _():
            arrived(6)

        @pl.when(mz != z)
        def _():
            @pl.when(r > 0)
            def _():
                adj_arrived(0).wait_recv()

            @pl.when(r < last)
            def _():
                adj_arrived(1).wait_recv()

            adj_pair_arrived().wait_recv()

        for mine in chunks:
            mine = [x for x in mine if x < xs]
            planes = [(x, f) for x in mine for f in range(fl)]
            result = smooth([
                jnp.concatenate([(ms[part, z, at_x(x) * fl + f] * adj[z, part])[None] for x, f in planes])
                for part in range(3)
            ])
            for j, (x, f) in enumerate(planes):
                fin[x, z, f] = result[j]
            for x in mine:
                if x:
                    fin_copy(x, z).start()
                else:
                    fin_own(z).start()

    add_others(0, 1)
    finish(0, 0)
    finish(0, 1)
    add_others(1, 0)
    increment(0)
    finish(1, 0)
    add_others(1, 1)
    finish(1, 1)
    increment(1)
    pl.when(mz == 0)(transport)
    pl.when(mz == 1)(transport)
    second(0, ((2, 1, 3, 0),))
    second(1, ((2, 1, 3, 0),))

    for z, half in pieces:
        for x in beside:
            pert_copy(x, z, half).wait_send()
        z_copy(z, half).wait_send()
    for x in beside:
        for field in range(fl):
            for z in range(2):
                smo_copy(x, field, z).wait_send()
    for number in range(len(nb)):
        sent(number)
    for number in range(2):
        pair_copy(number).wait_send()
    dep_copy.wait()
    for z in range(2):
        fin_own(z).wait()
        for x in beside:
            fin_copy(x, z).wait_send()
    for z in range(2):
        for x in beside:
            fin_copy(x, z).wait_recv()


def solution(mesh):
    regions = mesh.shape["region"]

    def shards(controls, perturbations, assignment, courant, innovation, obs_weight):
        fl, levels, height, columns = controls.shape
        kl = perturbations.shape[0]
        fields, xs = fl * levels, levels // 2
        vhi, vlo, coef = tables(columns)
        extent = height + 2 * HALO
        in_hbm = pl.BlockSpec(memory_space=pltpu.HBM)
        smem = pl.BlockSpec(memory_space=pltpu.SMEM)
        dma = pltpu.SemaphoreType.DMA
        lft, departure = pl.pallas_call(
            functools.partial(kernel, regions),
            out_shape=(
                pltpu.VMEM(controls.shape, F32),
                pltpu.VMEM(innovation.shape, F32),
            ),
            in_specs=[in_hbm, in_hbm, smem] + [in_hbm] * 6,
            out_specs=(pl.BlockSpec(memory_space=pl.ANY),) * 2,
            scratch_shapes=[
                pltpu.VMEM((columns, columns), BF16),
                pltpu.VMEM((columns, columns), BF16),
                pltpu.VMEM((PASSES + 1, GROUP, columns), F32),
                pltpu.VMEM((3, fl, levels, height, columns), F32),
                pltpu.VMEM((2, kl * xs, height, columns), F32),
                pltpu.VMEM((2, fields, height, columns), F32),
                pltpu.VMEM((2, fl * xs, height, columns), F32),
                pltpu.VMEM((fl, 2, xs, height, columns), F32),
                pltpu.VMEM((2, fl * xs, height, columns), F32),
                pltpu.VMEM((3, 2, fl * xs, height, columns), F32),
                pltpu.VMEM((2, extent, columns), F32),
                pltpu.VMEM((height, columns), F32),
                pltpu.VMEM((STEPS, 4, extent, columns), F32),
                pltpu.VMEM((extent, columns), F32),
                pltpu.VMEM((extent, columns), F32),
                pltpu.VMEM((2, 3, height, columns), F32),
                pltpu.VMEM((height, columns), F32),
                pltpu.VMEM((columns // 128, 3 * GROUP * height, 128), F32),
                pltpu.VMEM((3 * height, GROUP, columns), F32),
                pltpu.VMEM((columns // 128, GROUP * height, 128), F32),
                pltpu.VMEM((xs, 2, fl, height, columns), F32),
                dma((9,)),
                dma((4, 2, 2)),
                dma((4, 2, 2)),
                dma((2, 2)),
                dma((2, 2)),
                dma((12, 2)),
                dma((12, 2)),
                dma((2,)),
                dma((2,)),
                dma((4, fl, 2)),
                dma((4, fl, 2)),
                dma((4, 2)),
                dma((4, 2)),
                dma,
            ],
            compiler_params=pltpu.CompilerParams(
                collective_id=0, has_side_effects=True, vmem_limit_bytes=56 * 2**20
            ),
            cost_estimate=pl.CostEstimate(flops=2 * 10**9, bytes_accessed=8 * 2**20, transcendentals=0),
        )(controls, perturbations, assignment, courant, innovation, obs_weight, vhi, vlo, coef)
        return controls + lft, departure

    return jax.shard_map(
        shards,
        mesh=mesh,
        in_specs=(
            P("member", None, "region", None),
            P("member", None, "region", None),
            P(),
            P(None, None, "member", "region", None),
            P("member", "region", None),
            P("member", "region", None),
        ),
        out_specs=(P("member", None, "region", None), P("member", "region", None)),
        check_vma=False,
    )
```

```python
import functools

import jax
import jax.numpy as jnp
import numpy as np
from jax import lax
from jax.experimental import pallas as pl
from jax.experimental.pallas import tpu as pltpu
from jax.sharding import PartitionSpec as P

PASSES = 16
STEPS = 4
GROUP = 8
HALO = 8
MESH = pl.DeviceIdType.MESH
BESIDE = (1, 3, 2)
F32 = jnp.float32
BF16 = jnp.bfloat16


def tables(columns):
    index = np.arange(1, columns + 1, dtype=np.float64)
    sine = np.sqrt(2.0 / (columns + 1)) * np.sin(np.pi * np.outer(index, index) / (columns + 1))
    high = sine.astype(BF16)
    low = (sine - high.astype(np.float64)).astype(BF16)
    center = (1.0 + 2.0 * np.cos(np.pi * index / (columns + 1))) / 5.0
    power = np.ones((1, columns))
    for _ in range(PASSES):
        wider = np.zeros((power.shape[0] + 2, columns))
        wider[1:-1] += center * power
        wider[2:] += power / 5.0
        wider[:-2] += power / 5.0
        power = wider
    coef = np.broadcast_to(power[PASSES:, None, :], (PASSES + 1, GROUP, columns))
    return high, low, np.ascontiguousarray(coef).astype(np.float32)


def split(x):
    high = x.astype(BF16)
    return high, (x - high.astype(F32)).astype(BF16)


def times_sine(x, vhi, vlo):
    high, low = split(x)
    out = jnp.dot(high, vhi[...], preferred_element_type=F32)
    out += jnp.dot(low, vhi[...], preferred_element_type=F32)
    out += jnp.dot(high, vlo[...], preferred_element_type=F32)
    return out


def kernel(
    regions, ctl, pert, assign, cour, innov, weight, vhi_in, vlo_in, coef_in,
    lft, dep_out,
    vhi, vlo, coef, ctl3, pbuf, sums, home, smo_out, smo, ms, inc, inc_far, cour_x, inn_x, wgt_x, adj, dep,
    modes, rows, mid, fin,
    load_sem, pert_send, pert_recv, z_send, z_recv, nb_send, nb_recv, pair_send, pair_recv,
    smo_send, smo_recv, fin_send, fin_recv, out_sem,
):
    r, me = lax.axis_index("region"), lax.axis_index("member")
    fl, levels, height, columns = ctl.shape
    kl = pert.shape[0]
    xs = levels // 2
    part_fields = fl * xs
    groups = 2 * part_fields // GROUP
    tiles = columns // 128
    last = regions - 1
    mx, mz = lax.rem(me, xs), me // xs
    beside = [x for x in BESIDE if x < xs]

    def at_x(x):
        return lax.rem(mx + x, xs)

    def beside_me(x):
        return mz * xs + at_x(x)

    across = (1 - mz) * xs + mx

    barrier = pltpu.get_barrier_semaphore()
    for x in beside:
        pl.semaphore_signal(barrier, inc=1, device_id=(r, beside_me(x)), device_id_type=MESH)
    pl.semaphore_signal(barrier, inc=1, device_id=(r, across), device_id_type=MESH)

    @pl.when(r > 0)
    def _():
        for to in (me, across):
            pl.semaphore_signal(barrier, inc=1, device_id=(r - 1, to), device_id_type=MESH)

    @pl.when(r < last)
    def _():
        for to in (me, across):
            pl.semaphore_signal(barrier, inc=1, device_id=(r + 1, to), device_id_type=MESH)

    loads = [
        pltpu.make_async_copy(vhi_in, vhi, load_sem.at[0]),
        pltpu.make_async_copy(vlo_in, vlo, load_sem.at[1]),
        pltpu.make_async_copy(coef_in, coef, load_sem.at[2]),
        pltpu.make_async_copy(ctl, ctl3.at[1], load_sem.at[3]),
        pltpu.make_async_copy(pert.at[:, mx], pbuf.at[0, pl.ds(mx * kl, kl)], load_sem.at[4]),
        pltpu.make_async_copy(pert.at[:, xs + mx], pbuf.at[1, pl.ds(mx * kl, kl)], load_sem.at[5]),
        pltpu.make_async_copy(cour.at[:, :, 0], cour_x.at[:, :, pl.ds(HALO, height)], load_sem.at[6]),
        pltpu.make_async_copy(innov.at[0], inn_x.at[pl.ds(HALO, height)], load_sem.at[7]),
        pltpu.make_async_copy(weight.at[0], wgt_x.at[pl.ds(HALO, height)], load_sem.at[8]),
    ]
    for copy in loads:
        copy.start()

    top, bottom = pl.ds(0, HALO), pl.ds(height - HALO, HALO)
    above, below = pl.ds(0, HALO), pl.ds(HALO + height, HALO)
    halves = (top, bottom)
    nb = [
        ((ctl, ctl3.at[0]), (ctl, ctl3.at[2]), me),
        ((cour.at[:, :, 0, bottom], cour_x.at[:, :, above]), (cour.at[:, :, 0, top], cour_x.at[:, :, below]), me),
        ((innov.at[0, bottom], inn_x.at[above]), (innov.at[0, top], inn_x.at[below]), me),
        ((weight.at[0, bottom], wgt_x.at[above]), (weight.at[0, top], wgt_x.at[below]), me),
        ((inc.at[0, pl.ds(height, HALO)], inc.at[0, above]), (inc.at[0, pl.ds(HALO, HALO)], inc.at[0, below]), me),
        ((inc_far.at[bottom], inc.at[1, above]), (inc_far.at[top], inc.at[1, below]), across),
        ((adj.at[mz, 1], adj.at[mz, 0]), (adj.at[mz, 1], adj.at[mz, 2]), me),
        ((adj.at[mz, 1], adj.at[mz, 0]), (adj.at[mz, 1], adj.at[mz, 2]), across),
    ]
    pieces = [(z, half) for z in range(2) for half in range(2)]
    first_piece = len(nb)
    for z, half in pieces:
        own = ms.at[1, z, :, halves[half]]
        nb.append(((own, ms.at[0, z, :, halves[half]]), (own, ms.at[2, z, :, halves[half]]), me))

    def to_neighbour(number, up):
        src, dst = nb[number][up]
        return pltpu.make_async_remote_copy(
            src_ref=src, dst_ref=dst, send_sem=nb_send.at[number, up], recv_sem=nb_recv.at[number, up],
            device_id=(r - 1 if up else r + 1, nb[number][2]), device_id_type=MESH,
        )

    def exchange(number):
        @pl.when(r < last)
        def _():
            to_neighbour(number, 0).start()

        @pl.when(r > 0)
        def _():
            to_neighbour(number, 1).start()

    def arrived(number):
        @pl.when(r > 0)
        def _():
            to_neighbour(number, 0).wait_recv()

        @pl.when(r < last)
        def _():
            to_neighbour(number, 1).wait_recv()

    def sent(number):
        @pl.when(r < last)
        def _():
            to_neighbour(number, 0).wait_send()

        @pl.when(r > 0)
        def _():
            to_neighbour(number, 1).wait_send()

    def pair_copy(number):
        src, dst = ((inc_far, inc.at[1, pl.ds(HALO, height)]), (adj.at[mz, 1], adj.at[mz, 1]))[number]
        return pltpu.make_async_remote_copy(
            src_ref=src, dst_ref=dst, send_sem=pair_send.at[number], recv_sem=pair_recv.at[number],
            device_id=(r, across), device_id_type=MESH,
        )

    def pert_copy(x, z, half):
        return pltpu.make_async_remote_copy(
            src_ref=pert.at[:, z * xs + at_x(x), halves[half]], dst_ref=pbuf.at[z, pl.ds(mx * kl, kl), halves[half]],
            send_sem=pert_send.at[x, z, half], recv_sem=pert_recv.at[x, z, half],
            device_id=(r, beside_me(x)), device_id_type=MESH,
        )

    def z_copy(z, half):
        return pltpu.make_async_remote_copy(
            src_ref=sums.at[z, pl.ds((1 - mz) * part_fields, part_fields), halves[half]],
            dst_ref=home.at[z, :, halves[half]],
            send_sem=z_send.at[z, half], recv_sem=z_recv.at[z, half],
            device_id=(r, across), device_id_type=MESH,
        )

    def smo_copy(x, field, z):
        return pltpu.make_async_remote_copy(
            src_ref=smo_out.at[field, z, at_x(x)], dst_ref=smo.at[z, mx * fl + field],
            send_sem=smo_send.at[x, field, z], recv_sem=smo_recv.at[x, field, z],
            device_id=(r, beside_me(x)), device_id_type=MESH,
        )

    def smo_own(field, z):
        return pltpu.make_async_copy(smo_out.at[field, z, mx], smo.at[z, mx * fl + field], smo_send.at[0, field, z])

    def send_smoothed(field, z):
        for x in beside:
            smo_copy(x, field, z).start()
        smo_own(field, z).start()

    def fin_copy(x, z):
        return pltpu.make_async_remote_copy(
            src_ref=fin.at[x, z], dst_ref=lft.at[:, z * xs + mx],
            send_sem=fin_send.at[x, z], recv_sem=fin_recv.at[x, z],
            device_id=(r, beside_me(x)), device_id_type=MESH,
        )

    def fin_own(z):
        return pltpu.make_async_copy(fin.at[0, z], lft.at[:, z * xs + mx], fin_send.at[0, z])

    neighbours = (r > 0).astype(jnp.int32) + (r < last).astype(jnp.int32)
    pl.semaphore_wait(barrier, len(beside) + 1 + 2 * neighbours)

    exchange(0)
    def send_piece(z, half):
        for x in beside:
            pert_copy(x, z, half).start()

    for z, half in pieces[:2]:
        send_piece(z, half)
    for number in (1, 2, 3):
        exchange(number)

    @pl.when(r == 0)
    def _():
        for ref in (inn_x, wgt_x, inc.at[0], inc.at[1]):
            ref[0:HALO] = jnp.zeros((HALO, columns), F32)
        cour_x[:, :, 0:HALO] = jnp.zeros((STEPS, 4, HALO, columns), F32)

    @pl.when(r == last)
    def _():
        for ref in (inn_x, wgt_x, inc.at[0], inc.at[1]):
            ref[HALO + height :] = jnp.zeros((HALO, columns), F32)
        cour_x[:, :, HALO + height :] = jnp.zeros((STEPS, 4, HALO, columns), F32)

    def smooth(x):
        group = x[0].shape[0]
        flat = jnp.concatenate([part.reshape(group * height, columns) for part in x], axis=0)
        spectrum = times_sine(flat, vhi, vlo)
        for t in range(tiles):
            lane = slice(t * 128, (t + 1) * 128)
            modes[t, : 3 * group * height] = spectrum[:, lane]
            for part in range(3):
                for i in range(height):
                    rows[part * height + i, :group, lane] = modes[t, pl.ds(part * group * height + i, group, stride=height), :]

        @pl.when(r == 0)
        def _():
            rows[height - 1] = jnp.zeros((GROUP, columns), F32)
            for k in range(1, height):
                rows[height - 1 - k] = -rows[height - 1 + k]

        @pl.when(r == last)
        def _():
            rows[2 * height] = jnp.zeros((GROUP, columns), F32)
            for k in range(1, height):
                rows[2 * height + k] = -rows[2 * height - k]

        step = 8

        @pl.loop(0, tiles * (height // step))
        def _(it):
            t = lax.rem(it, tiles)
            lane = pl.ds(pl.multiple_of(t * 128, 128), 128)
            i = (it // tiles) * step
            g = [rows[i + j, :group, lane] for j in range(2 * PASSES + step)]
            total = [None] * step
            for d in range(PASSES + 1):
                c = coef[d, :group, lane]
                for j in range(step):
                    at = PASSES + j
                    term = c * g[at] if d == 0 else c * (g[at - d] + g[at + d])
                    total[j] = term if d == 0 else total[j] + term
            for j in range(step):
                mid[t, pl.ds(i + j, group, stride=height), :] = total[j]

        own = jnp.concatenate([mid[t, : group * height] for t in range(tiles)], axis=1)
        return times_sine(own, vhi, vlo).reshape(group, height, columns)

    def add_source(x, z, half, first):
        which = [assign[(mz * xs + x) * kl + k] for k in range(kl)]
        p = [pbuf[z, x * kl + k, halves[half]] for k in range(kl)]
        for l in range(2 * part_fields):
            terms = [jnp.where(which[k] == l, 1.0, 0.0) * p[k] for k in range(kl)]
            while len(terms) > 1:
                terms = [a + b for a, b in zip(terms[::2], terms[1::2])]
            sums[z, l, halves[half]] = terms[0] if first else sums[z, l, halves[half]] + terms[0]

    def add_others(z, half):
        for x in beside:
            pert_copy(x, z, half).wait_recv()
            add_source(at_x(xs - x), z, half, False)
        z_copy(z, half).start()

    def finish(z, half):
        z_copy(z, half).wait_recv()
        for l in range(part_fields):
            ms[1, z, l, halves[half]] = sums[z, mz * part_fields + l, halves[half]] + home[z, l, halves[half]]
        exchange(first_piece + pieces.index((z, half)))

    loads[4].wait()
    loads[5].wait()
    for z, half in pieces:
        add_source(mx, z, half, True)
    add_others(0, 0)
    send_piece(1, 0)

    for number in range(4):
        loads[number].wait()
    arrived(0)
    for q in range(groups):
        planes = [((q * GROUP + j) // levels, (q * GROUP + j) % levels) for j in range(GROUP)]
        result = smooth([
            jnp.concatenate([ctl3[part, field, level][None] for field, level in planes]) for part in range(3)
        ])
        for j, (field, level) in enumerate(planes):
            smo_out[field, level // xs, level % xs] = result[j]
        for field in range(q * GROUP // levels, (q + 1) * GROUP // levels):
            send_smoothed(field, 0)
    send_piece(1, 1)
    for field in range(fl):
        send_smoothed(field, 1)

    def increment(z):
        total = jnp.zeros((height, columns), F32)
        for x in (0, *beside):
            for field in range(fl):
                if x:
                    smo_copy(x, field, z).wait_recv()
                else:
                    smo_own(field, z).wait()
                l = at_x(xs - x) * fl + field
                total += smo[z, l] * ms[1, z, l]

        @pl.when(mz == z)
        def _():
            inc[0, HALO : HALO + height] = total
            exchange(4)

        @pl.when(mz != z)
        def _():
            inc_far[...] = total
            pair_copy(0).start()
            exchange(5)

    extent = height + 2 * HALO
    column = lax.broadcasted_iota(jnp.int32, (extent, columns), 1)

    def from_west(y):
        return jnp.where(column == 0, 0.0, pltpu.roll(y, 1, 1))

    def from_east(y):
        return jnp.where(column == columns - 1, 0.0, pltpu.roll(y, columns - 1, 1))

    def from_north(y):
        return pltpu.roll(y, 1, 0)

    def from_south(y):
        return pltpu.roll(y, extent - 1, 0)

    dep_copy = pltpu.make_async_copy(dep, dep_out.at[0], out_sem)

    def transport():
        for number in (6, 7, 8):
            loads[number].wait()
        for number in (1, 2, 3, 4, 5):
            arrived(number)
        pair_copy(0).wait_recv()
        state = inc[0] + inc[1]
        for s in range(STEPS):
            n, so, w, e = (cour_x[s, k] for k in range(4))
            state = (
                (1.0 - (n + so + w + e)) * state
                + n * from_north(state) + so * from_south(state) + w * from_west(state) + e * from_east(state)
            )
        state = wgt_x[...] * (state - inn_x[...])
        dep[...] = state[HALO : HALO + height]
        for s in range(STEPS - 1, -1, -1):
            n, so, w, e = (cour_x[s, k] for k in range(4))
            state = (
                (1.0 - (n + so + w + e)) * state
                + from_south(n * state) + from_north(so * state) + from_east(w * state) + from_west(e * state)
            )
        adj[mz, 1] = state[HALO : HALO + height]
        exchange(7)
        exchange(6)
        pair_copy(1).start()
        dep_copy.start()

    def adj_arrived(up):
        far = 1 - mz
        return pltpu.make_async_remote_copy(
            src_ref=adj.at[far, 1], dst_ref=adj.at[far, 2 if up else 0],
            send_sem=nb_send.at[7, up], recv_sem=nb_recv.at[7, up],
            device_id=(r - 1 if up else r + 1, across), device_id_type=MESH,
        )

    def adj_pair_arrived():
        return pltpu.make_async_remote_copy(
            src_ref=adj.at[1 - mz, 1], dst_ref=adj.at[1 - mz, 1], send_sem=pair_send.at[1], recv_sem=pair_recv.at[1],
            device_id=(r, across), device_id_type=MESH,
        )

    def second(z, chunks):
        for half in range(2):
            arrived(first_piece + pieces.index((z, half)))

        @pl.when(mz == z)
        def _():
            arrived(6)

        @pl.when(mz != z)
        def _():
            @pl.when(r > 0)
            def _():
                adj_arrived(0).wait_recv()

            @pl.when(r < last)
            def _():
                adj_arrived(1).wait_recv()

            adj_pair_arrived().wait_recv()

        for mine in chunks:
            mine = [x for x in mine if x < xs]
            planes = [(x, f) for x in mine for f in range(fl)]
            result = smooth([
                jnp.concatenate([(ms[part, z, at_x(x) * fl + f] * adj[z, part])[None] for x, f in planes])
                for part in range(3)
            ])
            for j, (x, f) in enumerate(planes):
                fin[x, z, f] = result[j]
            for x in mine:
                if x:
                    fin_copy(x, z).start()
                else:
                    fin_own(z).start()

    add_others(0, 1)
    finish(0, 0)
    finish(0, 1)
    add_others(1, 0)
    increment(0)
    finish(1, 0)
    add_others(1, 1)
    finish(1, 1)
    increment(1)
    transport()
    second(0, ((2, 1, 3, 0),))
    second(1, ((2, 1, 3, 0),))

    for z, half in pieces:
        for x in beside:
            pert_copy(x, z, half).wait_send()
        z_copy(z, half).wait_send()
    for x in beside:
        for field in range(fl):
            for z in range(2):
                smo_copy(x, field, z).wait_send()
    for number in range(len(nb)):
        sent(number)
    for number in range(2):
        pair_copy(number).wait_send()
    dep_copy.wait()
    for z in range(2):
        fin_own(z).wait()
        for x in beside:
            fin_copy(x, z).wait_send()
    for z in range(2):
        for x in beside:
            fin_copy(x, z).wait_recv()


def solution(mesh):
    regions = mesh.shape["region"]

    def shards(controls, perturbations, assignment, courant, innovation, obs_weight):
        fl, levels, height, columns = controls.shape
        kl = perturbations.shape[0]
        fields, xs = fl * levels, levels // 2
        vhi, vlo, coef = tables(columns)
        extent = height + 2 * HALO
        in_hbm = pl.BlockSpec(memory_space=pltpu.HBM)
        smem = pl.BlockSpec(memory_space=pltpu.SMEM)
        dma = pltpu.SemaphoreType.DMA
        lft, departure = pl.pallas_call(
            functools.partial(kernel, regions),
            out_shape=(
                pltpu.VMEM(controls.shape, F32),
                pltpu.VMEM(innovation.shape, F32),
            ),
            in_specs=[in_hbm, in_hbm, smem] + [in_hbm] * 6,
            out_specs=(pl.BlockSpec(memory_space=pl.ANY),) * 2,
            scratch_shapes=[
                pltpu.VMEM((columns, columns), BF16),
                pltpu.VMEM((columns, columns), BF16),
                pltpu.VMEM((PASSES + 1, GROUP, columns), F32),
                pltpu.VMEM((3, fl, levels, height, columns), F32),
                pltpu.VMEM((2, kl * xs, height, columns), F32),
                pltpu.VMEM((2, fields, height, columns), F32),
                pltpu.VMEM((2, fl * xs, height, columns), F32),
                pltpu.VMEM((fl, 2, xs, height, columns), F32),
                pltpu.VMEM((2, fl * xs, height, columns), F32),
                pltpu.VMEM((3, 2, fl * xs, height, columns), F32),
                pltpu.VMEM((2, extent, columns), F32),
                pltpu.VMEM((height, columns), F32),
                pltpu.VMEM((STEPS, 4, extent, columns), F32),
                pltpu.VMEM((extent, columns), F32),
                pltpu.VMEM((extent, columns), F32),
                pltpu.VMEM((2, 3, height, columns), F32),
                pltpu.VMEM((height, columns), F32),
                pltpu.VMEM((columns // 128, 3 * GROUP * height, 128), F32),
                pltpu.VMEM((3 * height, GROUP, columns), F32),
                pltpu.VMEM((columns // 128, GROUP * height, 128), F32),
                pltpu.VMEM((xs, 2, fl, height, columns), F32),
                dma((9,)),
                dma((4, 2, 2)),
                dma((4, 2, 2)),
                dma((2, 2)),
                dma((2, 2)),
                dma((12, 2)),
                dma((12, 2)),
                dma((2,)),
                dma((2,)),
                dma((4, fl, 2)),
                dma((4, fl, 2)),
                dma((4, 2)),
                dma((4, 2)),
                dma,
            ],
            compiler_params=pltpu.CompilerParams(
                collective_id=0, has_side_effects=True, vmem_limit_bytes=56 * 2**20
            ),
            cost_estimate=pl.CostEstimate(flops=2 * 10**9, bytes_accessed=8 * 2**20, transcendentals=0),
        )(controls, perturbations, assignment, courant, innovation, obs_weight, vhi, vlo, coef)
        return controls + lft, departure

    return jax.shard_map(
        shards,
        mesh=mesh,
        in_specs=(
            P("member", None, "region", None),
            P("member", None, "region", None),
            P(),
            P(None, None, "member", "region", None),
            P("member", "region", None),
            P("member", "region", None),
        ),
        out_specs=(P("member", None, "region", None), P("member", "region", None)),
        check_vma=False,
    )
```
